512 devices in a mesh: wide: 64 (over y, z), tensor: 8 (over x, core).
Axes of the slice: x: 4, y: 4, z: 16, core: 2. Of those that a mesh axis runs over, the one named last changes fastest.
Arguments:
- hidden: bfloat16 [256, 8192], P('wide', 'tensor'), may hold values from -6 to 6
- q_base: bfloat16 [256, 8192], P('wide', 'tensor'), may hold values from -14 to 14
- base_key: bfloat16 [256, 1024], P('wide', 'tensor'), may hold values from -6 to 6
- base_value: bfloat16 [256, 1024], P('wide', 'tensor'), may hold values from -6 to 6
- paged_key_cache: bfloat16 [2048, 128, 1024], P('wide', None, 'tensor'), may hold values from -6 to 6
- paged_value_cache: bfloat16 [2048, 128, 1024], P('wide', None, 'tensor'), may hold values from -6 to 6
- page_table: int32 [256, 8], P('wide'), may hold values from 0 to 31, as said below
- context_len: int32 [256], P('wide'), may hold values from 128 to 1024, as said below
- adapter_id: int32 [256], P('wide'), may hold values from 0 to 127
- adapter_slot: int32 [128], replicated, may hold values from 0 to 127, each once
- query_key_value_down: bfloat16 [128, 8192, 192], P('wide', 'tensor'), may hold values from -0.0625 to 0.0625
- query_up_weight: bfloat16 [128, 64, 8192], P('wide', None, 'tensor'), may hold values from -0.75 to 0.75
- key_up_weight: bfloat16 [128, 64, 1024], P('wide', None, 'tensor'), may hold values from -0.75 to 0.75
- value_up_weight: bfloat16 [128, 64, 1024], P('wide', None, 'tensor'), may hold values from -0.75 to 0.75
- output_down_weight: bfloat16 [128, 8192, 64], P('wide', 'tensor'), may hold values from -0.0625 to 0.0625
- output_up_weight: bfloat16 [128, 64, 8192], P('wide', None, 'tensor'), may hold values from -0.75 to 0.75
Outputs:
- attention: bfloat16 [256, 8192], P('wide', 'tensor')
- output_adapter_term: bfloat16 [256, 8192], P('wide', 'tensor')
The draws below stay inside these ranges and needn't reach their ends.
Inputs may be any that keep to these rules, and one draw needn't show every extreme that they name: `page_table`: the 8 entries of the rows of the 4 requests of one index of wide are distinct page numbers of that index's 32 pages. `context_len`: some request holds exactly 1024 positions.
All inputs are finite; a program needn't handle non-finite values.
Results may differ from the reference program's by a relative error of at most 0.01595.
Values may be sent and summed in bfloat16 or wider, within the bound.
No kernel may reach another device: no remote copies, remote signals or barrier semaphores. Data moves between devices by JAX's collectives and lax.ppermute only.
A program may use at most 64 MiB of HBM per device.

```python
import math
import jax
import jax.numpy as jnp
import numpy as np
from jax import lax

D = 8192
QUERY_HEADS = 64
KEY_VALUE_HEADS = 8
HEAD_SIZE = 128
ADAPTER_RANK = 64
REQ_DEV = 4
PAGE_POSITIONS = 128
MOST_PAGES = 8
ADAPTER_COUNT = 128
REQUEST_COUNT = 256
POOL = 32
TOTAL_PAGES = 2048


def draw_q_base(key, part):
    key = jax.random.fold_in(key, 1)
    random_noise = jnp.clip(jax.random.normal(jax.random.fold_in(key, 5), (REQUEST_COUNT, QUERY_HEADS * HEAD_SIZE), jnp.float32), -6.0, 6.0)
    gathered_values = random_noise
    return gathered_values.astype(jnp.bfloat16)


def draw_paged_key_cache(key, part):
    key = jax.random.fold_in(key, 2)
    random_noise = jnp.clip(jax.random.normal(jax.random.fold_in(key, 5), (TOTAL_PAGES, PAGE_POSITIONS, KEY_VALUE_HEADS * HEAD_SIZE), jnp.float32), -6.0, 6.0)
    gathered_values = random_noise
    return gathered_values.astype(jnp.bfloat16)


def draw_page_table(key, part):
    key = jax.random.fold_in(key, 3)
    blocks = REQUEST_COUNT // REQ_DEV
    gathered_keys = jax.random.split(key, blocks)
    orders = jax.vmap(lambda single: jax.random.permutation(single, POOL))(gathered_keys)
    return orders.reshape(REQUEST_COUNT, MOST_PAGES).astype(jnp.int32)


def draw_context_len(key, part):
    key = jax.random.fold_in(key, 4)
    lengths = jax.random.randint(key, (REQUEST_COUNT,), PAGE_POSITIONS, MOST_PAGES * PAGE_POSITIONS + 1)
    return lengths.at[0].set(MOST_PAGES * PAGE_POSITIONS).astype(jnp.int32)


def touch_ends(array, own_key, smallest, largest):
    longest = array.shape.index(max(array.shape))
    spots = []
    for shift in (0, 1):
        where = [jax.random.randint(jax.random.fold_in(own_key, axis), (), 0, length) for axis, length in enumerate(array.shape)]
        where[longest] = (where[longest] + shift) % array.shape[longest]
        spots.append(tuple(where))
    return array.at[spots[0]].set(smallest).at[spots[1]].set(largest)


def block_scale(rng, extent, cuts, smallest, high):
    def one(axis_at, blocks):
        steps = jax.random.uniform(jax.random.fold_in(jax.random.fold_in(rng, 6), axis_at), (blocks,), jnp.float32, smallest / len(cuts), high / len(cuts))
        return jnp.repeat(jnp.exp(steps), extent[axis_at] // blocks).reshape((-1,) + (1,) * (len(extent) - axis_at - 1))

    factor_of = one(*cuts[0])
    for cut in cuts[1:]:
        factor_of = factor_of * one(*cut)
    return factor_of


def rank_bounds(number_of, skew):
    loads = [(1 << 20) // math.isqrt(rank ** skew) + 1 for rank in range(1, number_of + 1)]
    scale = 1 + sum(loads) // (1 << 30)
    return np.cumsum(np.array([max(1, weight // scale) for weight in loads]))


def skewed_ids(rng, dims, count, lean):
    listing = rank_bounds(count, lean)
    pick = jax.random.randint(jax.random.fold_in(rng, 1), dims, 0, int(listing[count - 1]))
    grade = jnp.searchsorted(jnp.asarray(listing, jnp.int32), pick, side="right")
    return jax.random.permutation(jax.random.fold_in(rng, 2), count)[grade].astype(jnp.int32)


def gaussian(rng, dims, deviation, limit, cuts=(), kind=jnp.bfloat16):
    array = deviation * jax.random.normal(rng, dims, jnp.float32)
    if cuts:
        array = array * block_scale(rng, dims, cuts, -0.22, 0.18)
    return jnp.clip(array, -limit, limit).astype(kind)


def setup_inputs(seed: int = 0) -> dict:
    key_list = jax.random.split(jax.random.key(seed), 17)
    return {
        "hidden": gaussian(key_list[0], (REQUEST_COUNT, D), 1.0, 6.0, ((0, 64), (1, 8))),
        "q_base": draw_q_base(jax.random.fold_in(key_list[16], 71), 0),
        "base_key": gaussian(key_list[2], (REQUEST_COUNT, KEY_VALUE_HEADS * HEAD_SIZE), 1.0, 6.0, ((0, 64), (1, 8))),
        "base_value": gaussian(key_list[3], (REQUEST_COUNT, KEY_VALUE_HEADS * HEAD_SIZE), 1.0, 6.0, ((0, 64), (1, 8))),
        "paged_key_cache": draw_paged_key_cache(jax.random.fold_in(key_list[16], 71), 0),
        "paged_value_cache": gaussian(key_list[5], (TOTAL_PAGES, PAGE_POSITIONS, KEY_VALUE_HEADS * HEAD_SIZE), 1.0, 6.0, ((0, 64), (2, 8))),
        "page_table": draw_page_table(jax.random.fold_in(key_list[16], 71), 0),
        "context_len": draw_context_len(jax.random.fold_in(key_list[16], 71), 0),
        "adapter_id": touch_ends(skewed_ids(key_list[8], (REQUEST_COUNT,), ADAPTER_COUNT, 2), jax.random.fold_in(key_list[8], 3), 0, ADAPTER_COUNT - 1).astype(jnp.int32),
        "adapter_slot": jax.random.permutation(key_list[9], ADAPTER_COUNT).astype(jnp.int32),
        "query_key_value_down": gaussian(key_list[10], (ADAPTER_COUNT, D, 3 * ADAPTER_RANK), D ** -0.5, 0.0625, ((0, 64), (1, 8))),
        "query_up_weight": gaussian(key_list[11], (ADAPTER_COUNT, ADAPTER_RANK, QUERY_HEADS * HEAD_SIZE), ADAPTER_RANK ** -0.5, 0.75, ((0, 64), (2, 8))),
        "key_up_weight": gaussian(key_list[12], (ADAPTER_COUNT, ADAPTER_RANK, KEY_VALUE_HEADS * HEAD_SIZE), ADAPTER_RANK ** -0.5, 0.75, ((0, 64), (2, 8))),
        "value_up_weight": gaussian(key_list[13], (ADAPTER_COUNT, ADAPTER_RANK, KEY_VALUE_HEADS * HEAD_SIZE), ADAPTER_RANK ** -0.5, 0.75, ((0, 64), (2, 8))),
        "output_down_weight": gaussian(key_list[14], (ADAPTER_COUNT, QUERY_HEADS * HEAD_SIZE, ADAPTER_RANK), (QUERY_HEADS * HEAD_SIZE) ** -0.5, 0.0625, ((0, 64), (1, 8))),
        "output_up_weight": gaussian(key_list[15], (ADAPTER_COUNT, ADAPTER_RANK, D), ADAPTER_RANK ** -0.5, 0.75, ((0, 64), (2, 8))),
    }


adapter_scale = 2.0


def rounded_values(gathered_values):
    return lax.optimization_barrier(gathered_values.astype(jnp.bfloat16)).astype(jnp.float32)


def reference(hidden, q_base, base_key, base_value, paged_key_cache, paged_value_cache, page_table, context_len, adapter_id, adapter_slot, query_key_value_down, query_up_weight, key_up_weight, value_up_weight, output_down_weight, output_up_weight):
    slot_of = adapter_slot[adapter_id].astype(jnp.int32)
    inverse = 1.0 / (HEAD_SIZE ** 0.5)
    head_group = QUERY_HEADS // KEY_VALUE_HEADS
    request_numbers = jnp.arange(REQUEST_COUNT, dtype=jnp.int32)

    def expand(rank_row_values, up_weight_pages):
        return rounded_values(adapter_scale * jnp.dot(rank_row_values, up_weight_pages, preferred_element_type=jnp.float32))

    def one_request(items):
        hidden_row, single_query_row, cached_key_row, cached_value_row, request_pages, length, chosen_slots, request_number = items
        global_pages = (request_pages + (request_number // REQ_DEV) * POOL).astype(jnp.int32)
        ranks_qkv = jnp.dot(hidden_row[None, :], query_key_value_down[chosen_slots], preferred_element_type=jnp.float32).astype(jnp.bfloat16)
        query_delta = expand(ranks_qkv[:, 0:ADAPTER_RANK], query_up_weight[chosen_slots])
        key_delta = expand(ranks_qkv[:, ADAPTER_RANK:2 * ADAPTER_RANK], key_up_weight[chosen_slots])
        value_delta = expand(ranks_qkv[:, 2 * ADAPTER_RANK:3 * ADAPTER_RANK], value_up_weight[chosen_slots])
        query_vector = (single_query_row[None, :].astype(jnp.float32) + query_delta).astype(jnp.bfloat16).reshape(KEY_VALUE_HEADS, head_group, HEAD_SIZE)
        new_token_key = (cached_key_row[None, :].astype(jnp.float32) + key_delta).astype(jnp.bfloat16).reshape(KEY_VALUE_HEADS, HEAD_SIZE)
        new_token_value = (cached_value_row[None, :].astype(jnp.float32) + value_delta).astype(jnp.bfloat16).reshape(KEY_VALUE_HEADS, HEAD_SIZE)
        gathered_keys = paged_key_cache[global_pages].reshape(MOST_PAGES * PAGE_POSITIONS, KEY_VALUE_HEADS, HEAD_SIZE).astype(jnp.float32)
        gathered_values = paged_value_cache[global_pages].reshape(MOST_PAGES * PAGE_POSITIONS, KEY_VALUE_HEADS, HEAD_SIZE).astype(jnp.float32)
        query_wide = query_vector.astype(jnp.float32)
        scores = jnp.einsum("kgd,tkd->kgt", query_wide, gathered_keys) * inverse
        own_score = jnp.einsum("kgd,kd->kg", query_wide, new_token_key.astype(jnp.float32)) * inverse
        live = (jnp.arange(MOST_PAGES * PAGE_POSITIONS, dtype=jnp.int32) < length)[None, None, :]
        scores = jnp.where(live, scores, jnp.float32(-1e30))
        top = jnp.maximum(jnp.max(scores, axis=-1), own_score)
        weights = jnp.where(live, jnp.exp(scores - top[..., None]), jnp.float32(0.0))
        own_weight = jnp.exp(own_score - top)
        total = jnp.sum(weights, axis=-1) + own_weight
        mixed = jnp.einsum("kgt,tkd->kgd", rounded_values(weights), gathered_values)
        mixed = mixed + rounded_values(own_weight)[..., None] * new_token_value.astype(jnp.float32)[:, None, :]
        attention_row = (mixed / total[..., None]).reshape(QUERY_HEADS * HEAD_SIZE).astype(jnp.bfloat16)
        output_ranks = jnp.dot(attention_row[None, :], output_down_weight[chosen_slots], preferred_element_type=jnp.float32).astype(jnp.bfloat16)
        output_delta = (adapter_scale * jnp.dot(output_ranks, output_up_weight[chosen_slots], preferred_element_type=jnp.float32)).astype(jnp.bfloat16)
        return attention_row, output_delta[0]

    attention, output_adapter_term = lax.map(one_request, (hidden, q_base, base_key, base_value, page_table, context_len, slot_of, request_numbers))
    return attention, output_adapter_term
```

```python
import jax
import jax.numpy as jnp
import numpy as np
from jax import lax
from jax.sharding import Mesh, PartitionSpec as P

HEAD_SIZE = 128
adapter_scale = 2.0
Y, Z, T = "y", "z", "tensor"


def rounded_values(values):
    return lax.optimization_barrier(values.astype(jnp.bfloat16)).astype(jnp.float32)


def exchange(blocks, axis):
    return lax.all_to_all(blocks, axis, 0, 0)


def spread(block, axis):
    copies = jnp.broadcast_to(block[None], (lax.axis_size(axis),) + block.shape)
    return exchange(copies, axis)


def partial_ranks(rows, weight_pages, mask):
    product = jnp.einsum("nd,jdr->njr", rows, weight_pages, preferred_element_type=jnp.float32)
    return jnp.sum(product * mask[:, :, None], axis=1)


def summed(parts):
    return jnp.sum(parts.astype(jnp.float32), axis=0)


def up(ranks, weight_pages, mask):
    count, rank, width = weight_pages.shape
    picked = (ranks[:, None, :] * mask.astype(jnp.bfloat16)[:, :, None]).reshape(-1, count * rank)
    product = jnp.dot(
        picked, weight_pages.reshape(count * rank, width), preferred_element_type=jnp.float32
    )
    return (adapter_scale * product).astype(jnp.bfloat16)


def to_requests(rows):
    return summed(exchange(rows.reshape(lax.axis_size(Z), -1, rows.shape[1]), Z))


def body(
    hidden,
    q_base,
    base_key,
    base_value,
    paged_key_cache,
    paged_value_cache,
    page_table,
    context_len,
    adapter_id,
    adapter_slot,
    query_key_value_down,
    query_up_weight,
    key_up_weight,
    value_up_weight,
    output_down_weight,
    output_up_weight,
):
    local_rows, local_width = hidden.shape
    local_count = query_key_value_down.shape[0]
    lookup = jnp.arange(adapter_slot.shape[0], dtype=jnp.int32)
    own_slots = jnp.sum(
        jnp.where(adapter_id[:, None] == lookup[None, :], adapter_slot[None, :], 0), axis=1
    )
    tags = jnp.broadcast_to(own_slots.astype(jnp.bfloat16)[:, None], (local_rows, 128))
    column = [
        lax.all_gather(weight, Y, axis=0, tiled=True)
        for weight in (query_up_weight, key_up_weight, value_up_weight, output_down_weight, output_up_weight)
    ]
    y_size, z_size, t_size = lax.axis_size(Y), lax.axis_size(Z), lax.axis_size(T)
    z_rows = spread(jnp.concatenate([hidden, tags], axis=1), Z).reshape(z_size * local_rows, -1)
    all_rows = spread(z_rows, Y).reshape(y_size * z_size * local_rows, -1)

    numbers = jnp.arange(local_count, dtype=jnp.int32)
    first = lax.axis_index(Z) * local_count
    owned_slots = lax.axis_index(Y) * z_size * local_count + first + numbers
    column_slots = (
        jnp.arange(y_size, dtype=jnp.int32)[:, None] * (z_size * local_count) + first + numbers[None, :]
    ).reshape(-1)
    all_slots = all_rows[:, local_width].astype(jnp.int32)
    owned_mask = (all_slots[:, None] == owned_slots[None, :]).astype(jnp.float32)
    z_slots = z_rows[:, local_width].astype(jnp.int32)
    column_mask = (z_slots[:, None] == column_slots[None, :]).astype(jnp.float32)

    part = partial_ranks(all_rows[:, :local_width], query_key_value_down, owned_mask)
    share = z_size * local_rows // t_size
    shares = exchange(part.reshape(y_size * t_size, share, -1), (Y, T))
    ranks = spread(summed(shares).astype(jnp.bfloat16), T).reshape(z_size * local_rows, -1)
    width = query_up_weight.shape[1]
    delta = jnp.concatenate(
        [up(ranks[:, i * width : (i + 1) * width], column[i], column_mask) for i in range(3)],
        axis=1,
    )
    adapter_delta = to_requests(delta)
    width_q = q_base.shape[1]
    width_k = base_key.shape[1]
    query_vector = (q_base.astype(jnp.float32) + adapter_delta[:, 0:width_q]).astype(jnp.bfloat16)
    new_token_key = (
        base_key.astype(jnp.float32) + adapter_delta[:, width_q : width_q + width_k]
    ).astype(jnp.bfloat16)
    new_token_value = (
        base_value.astype(jnp.float32) + adapter_delta[:, width_q + width_k : width_q + 2 * width_k]
    ).astype(jnp.bfloat16)
    kv_local = width_k // HEAD_SIZE
    head_group = width_q // width_k
    gathered_keys = paged_key_cache[page_table].reshape(local_rows, -1, kv_local, HEAD_SIZE)
    gathered_values = paged_value_cache[page_table].reshape(local_rows, -1, kv_local, HEAD_SIZE)
    query_heads = query_vector.reshape(local_rows, kv_local, head_group, HEAD_SIZE)
    inverse = 1.0 / HEAD_SIZE**0.5
    scores = (
        jnp.einsum(
            "bkgd,btkd->bkgt", query_heads, gathered_keys, preferred_element_type=jnp.float32
        )
        * inverse
    )
    own_score = (
        jnp.einsum(
            "txvc,txc->txv",
            query_heads,
            new_token_key.reshape(local_rows, kv_local, HEAD_SIZE),
            preferred_element_type=jnp.float32,
        )
        * inverse
    )
    positions = jnp.arange(gathered_keys.shape[1], dtype=jnp.int32)
    live = (positions[None, :] < context_len[:, None])[:, None, None, :]
    scores = jnp.where(live, scores, jnp.float32(-1e30))
    top = jnp.maximum(jnp.max(scores, axis=-1), own_score)
    weights = jnp.where(live, jnp.exp(scores - top[..., None]), jnp.float32(0.0))
    own_weight = jnp.exp(own_score - top)
    total = jnp.sum(weights, axis=-1) + own_weight
    mixed = jnp.einsum(
        "bkgt,btkd->bkgd",
        weights.astype(jnp.bfloat16),
        gathered_values,
        preferred_element_type=jnp.float32,
    )
    fresh_wide = new_token_value.reshape(local_rows, kv_local, 1, HEAD_SIZE).astype(jnp.float32)
    mixed = mixed + rounded_values(own_weight)[..., None] * fresh_wide
    attention = (mixed / total[..., None]).reshape(local_rows, width_q).astype(jnp.bfloat16)
    out_rows = spread(attention, Z).reshape(z_size * local_rows, -1)
    out_ranks = summed(spread(partial_ranks(out_rows, column[3], column_mask), T))
    output_adapter_term = to_requests(up(out_ranks.astype(jnp.bfloat16), column[4], column_mask))
    return (attention, output_adapter_term.astype(jnp.bfloat16))


def solution(mesh):
    chips_y = 4
    wide, tensor = mesh.devices.shape
    devices = np.asarray(mesh.devices).reshape(chips_y, wide // chips_y, tensor)
    W = (Y, Z)
    return jax.shard_map(
        body,
        mesh=Mesh(devices, (Y, Z, T)),
        in_specs=(
            P(W, T),
            P(W, T),
            P(W, T),
            P(W, T),
            P(W, None, T),
            P(W, None, T),
            P(W, None),
            P(W),
            P(W),
            P(),
            P(W, T, None),
            P(W, None, T),
            P(W, None, T),
            P(W, None, T),
            P(W, T, None),
            P(W, None, T),
        ),
        out_specs=(P(W, T), P(W, T)),
        check_vma=False,
    )
```

```python
import jax
import jax.numpy as jnp
import numpy as np
from jax import lax
from jax.sharding import Mesh, PartitionSpec as P

HEAD_SIZE = 128
adapter_scale = 2.0
Y, Z, T = "y", "z", "tensor"


def rounded_values(values):
    return lax.optimization_barrier(values.astype(jnp.bfloat16)).astype(jnp.float32)


def exchange(blocks, axis):
    return lax.all_to_all(blocks, axis, 0, 0)


def spread(block, axis):
    copies = jnp.broadcast_to(block[None], (lax.axis_size(axis),) + block.shape)
    return exchange(copies, axis)


def partial_ranks(rows, weight_pages, mask):
    product = jnp.einsum("nd,jdr->njr", rows, weight_pages, preferred_element_type=jnp.float32)
    return jnp.sum(product * mask[:, :, None], axis=1)


def summed(parts):
    return jnp.sum(parts.astype(jnp.float32), axis=0)


def up(ranks, weight_pages, mask):
    count, rank, width = weight_pages.shape
    picked = (ranks[:, None, :] * mask.astype(jnp.bfloat16)[:, :, None]).reshape(-1, count * rank)
    product = jnp.dot(
        picked, weight_pages.reshape(count * rank, width), preferred_element_type=jnp.float32
    )
    return (adapter_scale * product).astype(jnp.bfloat16)


def to_requests(rows):
    return summed(exchange(rows.reshape(lax.axis_size(Z), -1, rows.shape[1]), Z))


def body(
    hidden,
    q_base,
    base_key,
    base_value,
    paged_key_cache,
    paged_value_cache,
    page_table,
    context_len,
    adapter_id,
    adapter_slot,
    query_key_value_down,
    query_up_weight,
    key_up_weight,
    value_up_weight,
    output_down_weight,
    output_up_weight,
):
    local_rows, local_width = hidden.shape
    local_count = query_key_value_down.shape[0]
    lookup = jnp.arange(adapter_slot.shape[0], dtype=jnp.int32)
    own_slots = jnp.sum(
        jnp.where(adapter_id[:, None] == lookup[None, :], adapter_slot[None, :], 0), axis=1
    )
    tags = jnp.broadcast_to(own_slots.astype(jnp.bfloat16)[:, None], (local_rows, 128))
    y_size, z_size = lax.axis_size(Y), lax.axis_size(Z)
    pages = [query_key_value_down] + [
        lax.ppermute(query_key_value_down, Y, [(i, (i + k) % y_size) for i in range(y_size)])
        for k in range(1, y_size)
    ]
    up_weights = jnp.concatenate([query_up_weight, key_up_weight, value_up_weight], axis=2)
    column_up, column_out_down, column_out_up = [
        lax.all_gather(weight, Y, axis=0, tiled=True)
        for weight in (up_weights, output_down_weight, output_up_weight)
    ]
    z_rows = spread(jnp.concatenate([hidden, tags], axis=1), Z).reshape(z_size * local_rows, -1)
    z_slots = z_rows[:, local_width].astype(jnp.int32)
    own_y = lax.axis_index(Y)

    def mask_of(y):
        numbers = jnp.arange(local_count, dtype=jnp.int32)
        slots = (y[:, None] * z_size + lax.axis_index(Z)) * local_count + numbers[None, :]
        return (z_slots[:, None] == slots.reshape(-1)[None, :]).astype(jnp.float32)

    places = jnp.arange(y_size, dtype=jnp.int32)
    column_mask = mask_of(places)
    shifted_mask = mask_of((own_y - places) % y_size)
    part = sum(
        partial_ranks(
            z_rows[:, :local_width], page, shifted_mask[:, k * local_count : (k + 1) * local_count]
        )
        for k, page in enumerate(pages)
    )
    ranks = summed(spread(part, T)).astype(jnp.bfloat16)
    width, width_q, width_k = query_up_weight.shape[1], q_base.shape[1], base_key.shape[1]
    cuts = (0, width_q, width_q + width_k, width_q + 2 * width_k)
    delta = jnp.concatenate(
        [
            up(
                ranks[:, i * width : (i + 1) * width],
                column_up[:, :, cuts[i] : cuts[i + 1]],
                column_mask,
            )
            for i in range(3)
        ],
        axis=1,
    )
    adapter_delta = to_requests(delta)
    width_q = q_base.shape[1]
    width_k = base_key.shape[1]
    query_vector = (q_base.astype(jnp.float32) + adapter_delta[:, 0:width_q]).astype(jnp.bfloat16)
    new_token_key = (
        base_key.astype(jnp.float32) + adapter_delta[:, width_q : width_q + width_k]
    ).astype(jnp.bfloat16)
    new_token_value = (
        base_value.astype(jnp.float32) + adapter_delta[:, width_q + width_k : width_q + 2 * width_k]
    ).astype(jnp.bfloat16)
    kv_local = width_k // HEAD_SIZE
    head_group = width_q // width_k
    gathered_keys = paged_key_cache[page_table].reshape(local_rows, -1, kv_local, HEAD_SIZE)
    gathered_values = paged_value_cache[page_table].reshape(local_rows, -1, kv_local, HEAD_SIZE)
    query_heads = query_vector.reshape(local_rows, kv_local, head_group, HEAD_SIZE)
    inverse = 1.0 / HEAD_SIZE**0.5
    scores = (
        jnp.einsum(
            "bkgd,btkd->bkgt", query_heads, gathered_keys, preferred_element_type=jnp.float32
        )
        * inverse
    )
    own_score = (
        jnp.einsum(
            "txvc,txc->txv",
            query_heads,
            new_token_key.reshape(local_rows, kv_local, HEAD_SIZE),
            preferred_element_type=jnp.float32,
        )
        * inverse
    )
    positions = jnp.arange(gathered_keys.shape[1], dtype=jnp.int32)
    live = (positions[None, :] < context_len[:, None])[:, None, None, :]
    scores = jnp.where(live, scores, jnp.float32(-1e30))
    top = jnp.maximum(jnp.max(scores, axis=-1), own_score)
    weights = jnp.where(live, jnp.exp(scores - top[..., None]), jnp.float32(0.0))
    own_weight = jnp.exp(own_score - top)
    total = jnp.sum(weights, axis=-1) + own_weight
    mixed = jnp.einsum(
        "bkgt,btkd->bkgd",
        weights.astype(jnp.bfloat16),
        gathered_values,
        preferred_element_type=jnp.float32,
    )
    fresh_wide = new_token_value.reshape(local_rows, kv_local, 1, HEAD_SIZE).astype(jnp.float32)
    mixed = mixed + rounded_values(own_weight)[..., None] * fresh_wide
    attention = (mixed / total[..., None]).reshape(local_rows, width_q).astype(jnp.bfloat16)
    out_rows = spread(attention, Z).reshape(z_size * local_rows, -1)
    out_ranks = summed(spread(partial_ranks(out_rows, column_out_down, column_mask), T))
    output_adapter_term = to_requests(up(out_ranks.astype(jnp.bfloat16), column_out_up, column_mask))
    return (attention, output_adapter_term.astype(jnp.bfloat16))


def solution(mesh):
    chips_y = 4
    wide, tensor = mesh.devices.shape
    devices = np.asarray(mesh.devices).reshape(chips_y, wide // chips_y, tensor)
    W = (Y, Z)
    return jax.shard_map(
        body,
        mesh=Mesh(devices, (Y, Z, T)),
        in_specs=(
            P(W, T),
            P(W, T),
            P(W, T),
            P(W, T),
            P(W, None, T),
            P(W, None, T),
            P(W, None),
            P(W),
            P(W),
            P(),
            P(W, T, None),
            P(W, None, T),
            P(W, None, T),
            P(W, None, T),
            P(W, T, None),
            P(W, None, T),
        ),
        out_specs=(P(W, T), P(W, T)),
        check_vma=False,
    )
```

```python
import jax
import jax.numpy as jnp
import numpy as np
from jax import lax
from jax.experimental import pallas as pl
from jax.experimental.pallas import tpu as pltpu
from jax.sharding import Mesh, PartitionSpec as P

HEAD_SIZE = 128
adapter_scale = 2.0
Y, Z, T = "y", "z", "tensor"


def rounded_values(values):
    return lax.optimization_barrier(values.astype(jnp.bfloat16)).astype(jnp.float32)


def exchange(blocks, axis):
    return lax.all_to_all(blocks, axis, 0, 0)


def spread(block, axis):
    copies = jnp.broadcast_to(block[None], (lax.axis_size(axis),) + block.shape)
    return exchange(copies, axis)


def summed(parts):
    return jnp.sum(parts.astype(jnp.float32), axis=0)


NT = (((1,), (1,)), ((), ()))
VMEM = pl.BlockSpec(memory_space=pltpu.VMEM)
SMEM = pl.BlockSpec(memory_space=pltpu.SMEM)


def call(kernel, shape, dtype, *operands):
    return pl.pallas_call(
        kernel,
        out_shape=jax.ShapeDtypeStruct(shape, dtype),
        in_specs=[SMEM] + [VMEM] * (len(operands) - 1),
        out_specs=VMEM,
        compiler_params=pltpu.CompilerParams(vmem_limit_bytes=40 * 2**20),
    )(*operands)


def pack(slots_ref, *refs):
    out_ref, at = refs[-1], 0
    for ref in refs[:-1]:
        out_ref[:, :, at : at + ref.shape[2]] = ref[...]
        at += ref.shape[2]


def picked(slots_ref, tags, values, number):
    return jnp.where(tags == slots_ref[number].astype(jnp.float32), values, jnp.zeros_like(values))


def tags_of(rows_ref, at, width):
    return rows_ref[:, at : at + width].astype(jnp.float32)


def grown(slots_ref, tags, ranks, pages, at, width):
    total = None
    for k, page in enumerate(pages):
        count, rank, _ = page.shape
        mine = [picked(slots_ref, tags, ranks, k * count + j) for j in range(count)]
        product = jnp.dot(
            jnp.concatenate(mine, axis=1).astype(jnp.bfloat16),
            page[:, :, at : at + width].reshape(count * rank, width),
            preferred_element_type=jnp.float32,
        )
        total = product if total is None else total + product
    return (adapter_scale * total).astype(jnp.bfloat16)


def make_up_first(cuts):
    def up_first(slots_ref, ranks_ref, rows_ref, *refs):
        pages, out_ref = refs[:-1], refs[-1]
        rank = pages[0].shape[1]
        tags = tags_of(rows_ref, rows_ref.shape[1] - 128, rank)
        ranks = ranks_ref[...].astype(jnp.float32)
        for i in range(3):
            out_ref[:, cuts[i] : cuts[i + 1]] = grown(
                slots_ref,
                tags,
                ranks[:, i * rank : (i + 1) * rank],
                pages,
                cuts[i],
                cuts[i + 1] - cuts[i],
            )

    return up_first


def make_down_second(at):
    def down_second(slots_ref, out_rows_ref, rows_ref, *refs):
        pages, out_ref = refs[:-1], refs[-1]
        count, rank, _ = pages[0].shape
        rows = out_rows_ref[...]
        tags = tags_of(rows_ref, rows_ref.shape[1] - 128, rank)
        total = jnp.zeros((rows.shape[0], rank), jnp.float32)
        for k, page in enumerate(pages):
            for j in range(count):
                weight = page[j, :, at : at + rows.shape[1]]
                product = lax.dot_general(rows, weight, NT, preferred_element_type=jnp.float32)
                total = total + picked(slots_ref, tags, product, k * count + j)
        half = rows.shape[0] // 2
        side = jnp.concatenate([total[:half], total[half:]], axis=1)
        for t in range(out_ref.shape[0]):
            out_ref[t] = side

    return down_second


def make_up_second(at):
    def up_second(slots_ref, parts_ref, rows_ref, *refs):
        pages, out_ref = refs[:-1], refs[-1]
        rank = pages[0].shape[1]
        side = jnp.sum(parts_ref[...], axis=0).astype(jnp.bfloat16).astype(jnp.float32)
        ranks = jnp.concatenate([side[:, :rank], side[:, rank:]], axis=0)
        tags = tags_of(rows_ref, rows_ref.shape[1] - 128, rank)
        out_ref[...] = grown(slots_ref, tags, ranks, pages, at, out_ref.shape[1])

    return up_second


def to_requests(rows):
    return summed(exchange(rows.reshape(lax.axis_size(Z), -1, rows.shape[1]), Z))


def body(
    hidden,
    q_base,
    base_key,
    base_value,
    paged_key_cache,
    paged_value_cache,
    page_table,
    context_len,
    adapter_id,
    adapter_slot,
    query_key_value_down,
    query_up_weight,
    key_up_weight,
    value_up_weight,
    output_down_weight,
    output_up_weight,
):
    local_rows, local_width = hidden.shape
    local_count = query_key_value_down.shape[0]
    lookup = jnp.arange(adapter_slot.shape[0], dtype=jnp.int32)
    own_slots = jnp.sum(
        jnp.where(adapter_id[:, None] == lookup[None, :], adapter_slot[None, :], 0), axis=1
    )
    tags = jnp.broadcast_to(own_slots.astype(jnp.bfloat16)[:, None], (local_rows, 128))
    y_size, z_size, t_size = lax.axis_size(Y), lax.axis_size(Z), lax.axis_size(T)
    rank, width_q, width_k = query_up_weight.shape[1], q_base.shape[1], base_key.shape[1]
    cuts = (0, width_q, width_q + width_k, width_q + 2 * width_k)
    own_y = lax.axis_index(Y)
    places = jnp.arange(y_size, dtype=jnp.int32)
    numbers = jnp.arange(local_count, dtype=jnp.int32)
    column_slots = (
        ((own_y - places[:, None]) % y_size * z_size + lax.axis_index(Z)) * local_count + numbers
    ).reshape(-1)
    packed_width = cuts[3] + local_width + output_up_weight.shape[2]
    packed = call(
        pack,
        (local_count, rank, packed_width),
        jnp.bfloat16,
        column_slots,
        query_up_weight,
        key_up_weight,
        value_up_weight,
        jnp.swapaxes(output_down_weight, 1, 2),
        output_up_weight,
    )
    pages = [packed] + [
        lax.ppermute(packed, Y, [(i, (i + k) % y_size) for i in range(y_size)])
        for k in range(1, y_size)
    ]
    z_rows = spread(jnp.concatenate([hidden, tags], axis=1), Z).reshape(z_size * local_rows, -1)
    all_rows = spread(z_rows, Y).reshape(y_size * z_size * local_rows, -1)

    all_slots = all_rows[:, local_width].astype(jnp.int32)
    owned_mask = (all_slots[:, None] == column_slots[None, :local_count]).astype(jnp.float32)
    product = jnp.einsum(
        "nd,jdr->njr",
        all_rows[:, :local_width],
        query_key_value_down,
        preferred_element_type=jnp.float32,
    )
    part = jnp.sum(product * owned_mask[:, :, None], axis=1)
    share = z_size * local_rows // t_size
    shares = exchange(part.reshape(y_size * t_size, share, -1), (Y, T))
    ranks = spread(summed(shares).astype(jnp.bfloat16), T).reshape(z_size * local_rows, -1)
    delta = call(
        make_up_first(cuts),
        (z_size * local_rows, cuts[3]),
        jnp.bfloat16,
        column_slots,
        ranks,
        z_rows,
        *pages,
    )
    adapter_delta = to_requests(delta)
    width_q = q_base.shape[1]
    width_k = base_key.shape[1]
    query_vector = (q_base.astype(jnp.float32) + adapter_delta[:, 0:width_q]).astype(jnp.bfloat16)
    new_token_key = (
        base_key.astype(jnp.float32) + adapter_delta[:, width_q : width_q + width_k]
    ).astype(jnp.bfloat16)
    new_token_value = (
        base_value.astype(jnp.float32) + adapter_delta[:, width_q + width_k : width_q + 2 * width_k]
    ).astype(jnp.bfloat16)
    kv_local = width_k // HEAD_SIZE
    head_group = width_q // width_k
    gathered_keys = paged_key_cache[page_table].reshape(local_rows, -1, kv_local, HEAD_SIZE)
    gathered_values = paged_value_cache[page_table].reshape(local_rows, -1, kv_local, HEAD_SIZE)
    query_heads = query_vector.reshape(local_rows, kv_local, head_group, HEAD_SIZE)
    inverse = 1.0 / HEAD_SIZE**0.5
    scores = (
        jnp.einsum(
            "bkgd,btkd->bkgt", query_heads, gathered_keys, preferred_element_type=jnp.float32
        )
        * inverse
    )
    own_score = (
        jnp.einsum(
            "txvc,txc->txv",
            query_heads,
            new_token_key.reshape(local_rows, kv_local, HEAD_SIZE),
            preferred_element_type=jnp.float32,
        )
        * inverse
    )
    positions = jnp.arange(gathered_keys.shape[1], dtype=jnp.int32)
    live = (positions[None, :] < context_len[:, None])[:, None, None, :]
    scores = jnp.where(live, scores, jnp.float32(-1e30))
    top = jnp.maximum(jnp.max(scores, axis=-1), own_score)
    weights = jnp.where(live, jnp.exp(scores - top[..., None]), jnp.float32(0.0))
    own_weight = jnp.exp(own_score - top)
    total = jnp.sum(weights, axis=-1) + own_weight
    mixed = jnp.einsum(
        "bkgt,btkd->bkgd",
        weights.astype(jnp.bfloat16),
        gathered_values,
        preferred_element_type=jnp.float32,
    )
    fresh_wide = new_token_value.reshape(local_rows, kv_local, 1, HEAD_SIZE).astype(jnp.float32)
    mixed = mixed + rounded_values(own_weight)[..., None] * fresh_wide
    attention = (mixed / total[..., None]).reshape(local_rows, width_q).astype(jnp.bfloat16)
    out_rows = spread(attention, Z).reshape(z_size * local_rows, -1)
    sides = call(
        make_down_second(cuts[3]),
        (t_size, z_size * local_rows // 2, 2 * rank),
        jnp.float32,
        column_slots,
        out_rows,
        z_rows,
        *pages,
    )
    term = call(
        make_up_second(cuts[3] + local_width),
        (z_size * local_rows, output_up_weight.shape[2]),
        jnp.bfloat16,
        column_slots,
        exchange(sides, T),
        z_rows,
        *pages,
    )
    output_adapter_term = to_requests(term)
    return (attention, output_adapter_term.astype(jnp.bfloat16))


def solution(mesh):
    chips_y = 4
    wide, tensor = mesh.devices.shape
    devices = np.asarray(mesh.devices).reshape(chips_y, wide // chips_y, tensor)
    W = (Y, Z)
    return jax.shard_map(
        body,
        mesh=Mesh(devices, (Y, Z, T)),
        in_specs=(
            P(W, T),
            P(W, T),
            P(W, T),
            P(W, T),
            P(W, None, T),
            P(W, None, T),
            P(W, None),
            P(W),
            P(W),
            P(),
            P(W, T, None),
            P(W, None, T),
            P(W, None, T),
            P(W, None, T),
            P(W, T, None),
            P(W, None, T),
        ),
        out_specs=(P(W, T), P(W, T)),
        check_vma=False,
    )
```

```python
import jax
import jax.numpy as jnp
import numpy as np
from jax import lax
from jax.experimental import pallas as pl
from jax.experimental.pallas import tpu as pltpu
from jax.sharding import Mesh, PartitionSpec as P

HEAD_SIZE = 128
adapter_scale = 2.0
Y, Z, T = "y", "z", "tensor"


def rounded_values(values):
    return lax.optimization_barrier(values.astype(jnp.bfloat16)).astype(jnp.float32)


def exchange(blocks, axis):
    return lax.all_to_all(blocks, axis, 0, 0)


def spread(block, axis):
    copies = jnp.broadcast_to(block[None], (lax.axis_size(axis),) + block.shape)
    return exchange(copies, axis)


def summed(parts):
    return jnp.sum(parts.astype(jnp.float32), axis=0)


NT = (((1,), (1,)), ((), ()))
VMEM = pl.BlockSpec(memory_space=pltpu.VMEM)
SMEM = pl.BlockSpec(memory_space=pltpu.SMEM)


def call(kernel, shape, dtype, *operands, scalars=1, after=()):
    count = len(operands)

    def body(*refs):
        kernel(*refs[:count], *refs[count + len(after) :])

    return pl.pallas_call(
        body,
        out_shape=jax.ShapeDtypeStruct(shape, dtype),
        in_specs=[SMEM] * scalars
        + [VMEM] * (count - scalars)
        + [pl.BlockSpec(memory_space=pl.ANY)] * len(after),
        out_specs=VMEM,
        compiler_params=pltpu.CompilerParams(vmem_limit_bytes=32 * 2**20),
    )(*operands, *after)


def first_blocks(id_ref, slot_ref, hidden_ref, out_ref):
    rows, width = hidden_ref.shape
    tags = [
        jnp.full((1, 128), slot_ref[id_ref[r]].astype(jnp.float32), jnp.float32) for r in range(rows)
    ]
    block = jnp.concatenate(
        [hidden_ref[...], jnp.concatenate(tags, axis=0).astype(jnp.bfloat16)], axis=1
    )
    for z in range(out_ref.shape[0]):
        out_ref[z] = block


def second_blocks(from_z_ref, out_ref):
    rows = from_z_ref[...].reshape(out_ref.shape[1:])
    for y in range(out_ref.shape[0]):
        out_ref[y] = rows


def pack(*refs):
    out_ref, at = refs[-1], 0
    for ref in refs[:-1]:
        out_ref[:, :, at : at + ref.shape[2]] = ref[...]
        at += ref.shape[2]


def picked(slots_ref, tags, values, number):
    return jnp.where(tags == slots_ref[number].astype(jnp.float32), values, jnp.zeros_like(values))


def tags_of(rows_ref, at, width):
    return rows_ref[:, at : at + width].astype(jnp.float32)


def grown(slots_ref, tags, ranks, pages, at, width):
    total = None
    for k, page in enumerate(pages):
        count, rank, _ = page.shape
        mine = [picked(slots_ref, tags, ranks, k * count + j) for j in range(count)]
        product = jnp.dot(
            jnp.concatenate(mine, axis=1).astype(jnp.bfloat16),
            page[:, :, at : at + width].reshape(count * rank, width),
            preferred_element_type=jnp.float32,
        )
        total = product if total is None else total + product
    return (adapter_scale * total).astype(jnp.bfloat16)


def make_up_first(cuts):
    def up_first(slots_ref, ranks_ref, rows_ref, *refs):
        pages, out_ref = refs[:-1], refs[-1]
        rank = pages[0].shape[1]
        tags = tags_of(rows_ref, rows_ref.shape[1] - 128, rank)
        ranks = ranks_ref[...].astype(jnp.float32)
        for i in range(3):
            out_ref[:, cuts[i] : cuts[i + 1]] = grown(
                slots_ref,
                tags,
                ranks[:, i * rank : (i + 1) * rank],
                pages,
                cuts[i],
                cuts[i + 1] - cuts[i],
            )

    return up_first


def make_down_second(at):
    def down_second(slots_ref, out_rows_ref, rows_ref, *refs):
        pages, out_ref = refs[:-1], refs[-1]
        count, rank, _ = pages[0].shape
        rows = out_rows_ref[...]
        tags = tags_of(rows_ref, rows_ref.shape[1] - 128, rank)
        total = jnp.zeros((rows.shape[0], rank), jnp.float32)
        for k, page in enumerate(pages):
            for j in range(count):
                weight = page[j, :, at : at + rows.shape[1]]
                product = lax.dot_general(rows, weight, NT, preferred_element_type=jnp.float32)
                total = total + picked(slots_ref, tags, product, k * count + j)
        half = rows.shape[0] // 2
        side = jnp.concatenate([total[:half], total[half:]], axis=1)
        for t in range(out_ref.shape[0]):
            out_ref[t] = side

    return down_second


def make_up_second(at):
    def up_second(slots_ref, parts_ref, rows_ref, *refs):
        pages, out_ref = refs[:-1], refs[-1]
        rank = pages[0].shape[1]
        side = jnp.sum(parts_ref[...], axis=0).astype(jnp.bfloat16).astype(jnp.float32)
        ranks = jnp.concatenate([side[:, :rank], side[:, rank:]], axis=0)
        tags = tags_of(rows_ref, rows_ref.shape[1] - 128, rank)
        out_ref[...] = grown(slots_ref, tags, ranks, pages, at, out_ref.shape[1])

    return up_second


def to_requests(rows):
    return summed(exchange(rows.reshape(lax.axis_size(Z), -1, rows.shape[1]), Z))


def body(
    hidden,
    q_base,
    base_key,
    base_value,
    paged_key_cache,
    paged_value_cache,
    page_table,
    context_len,
    adapter_id,
    adapter_slot,
    query_key_value_down,
    query_up_weight,
    key_up_weight,
    value_up_weight,
    output_down_weight,
    output_up_weight,
):
    local_rows, local_width = hidden.shape
    local_count = query_key_value_down.shape[0]
    y_size, z_size, t_size = lax.axis_size(Y), lax.axis_size(Z), lax.axis_size(T)
    rank, width_q, width_k = query_up_weight.shape[1], q_base.shape[1], base_key.shape[1]
    cuts = (0, width_q, width_q + width_k, width_q + 2 * width_k)
    own_y = lax.axis_index(Y)
    places = jnp.arange(y_size, dtype=jnp.int32)
    numbers = jnp.arange(local_count, dtype=jnp.int32)
    column_slots = (
        ((own_y - places[:, None]) % y_size * z_size + lax.axis_index(Z)) * local_count + numbers
    ).reshape(-1)

    def packed(*weights, after=()):
        width = sum(weight.shape[2] for weight in weights)
        shape = (local_count, rank, width)
        mine = call(pack, shape, jnp.bfloat16, *weights, scalars=0, after=after)
        return [mine] + [
            lax.ppermute(mine, Y, [(i, (i + k) % y_size) for i in range(y_size)])
            for k in range(1, y_size)
        ]

    up_pages = packed(query_up_weight, key_up_weight, value_up_weight)
    z_blocks = call(
        first_blocks,
        (z_size, local_rows, local_width + 128),
        jnp.bfloat16,
        adapter_id,
        adapter_slot,
        hidden,
        scalars=2,
    )
    y_blocks = call(
        second_blocks,
        (y_size, z_size * local_rows, local_width + 128),
        jnp.bfloat16,
        exchange(z_blocks, Z),
        scalars=0,
        after=up_pages[1:],
    )
    z_rows = y_blocks[0]
    all_rows = exchange(y_blocks, Y).reshape(y_size * z_size * local_rows, -1)

    all_slots = all_rows[:, local_width].astype(jnp.int32)
    owned_mask = (all_slots[:, None] == column_slots[None, :local_count]).astype(jnp.float32)
    product = jnp.einsum(
        "nd,jdr->njr",
        all_rows[:, :local_width],
        query_key_value_down,
        preferred_element_type=jnp.float32,
    )
    part = jnp.sum(product * owned_mask[:, :, None], axis=1)
    share = z_size * local_rows // t_size
    shares = exchange(part.reshape(y_size * t_size, share, -1), (Y, T))
    ranks = spread(summed(shares).astype(jnp.bfloat16), T).reshape(z_size * local_rows, -1)
    delta = call(
        make_up_first(cuts),
        (z_size * local_rows, cuts[3]),
        jnp.bfloat16,
        column_slots,
        ranks,
        z_rows,
        *up_pages,
    )
    out_pages = packed(
        jnp.swapaxes(output_down_weight, 1, 2), output_up_weight, after=(shares,)
    )
    adapter_delta = to_requests(delta)
    width_q = q_base.shape[1]
    width_k = base_key.shape[1]
    query_vector = (q_base.astype(jnp.float32) + adapter_delta[:, 0:width_q]).astype(jnp.bfloat16)
    new_token_key = (
        base_key.astype(jnp.float32) + adapter_delta[:, width_q : width_q + width_k]
    ).astype(jnp.bfloat16)
    new_token_value = (
        base_value.astype(jnp.float32) + adapter_delta[:, width_q + width_k : width_q + 2 * width_k]
    ).astype(jnp.bfloat16)
    kv_local = width_k // HEAD_SIZE
    head_group = width_q // width_k
    gathered_keys = paged_key_cache[page_table].reshape(local_rows, -1, kv_local, HEAD_SIZE)
    gathered_values = paged_value_cache[page_table].reshape(local_rows, -1, kv_local, HEAD_SIZE)
    query_heads = query_vector.reshape(local_rows, kv_local, head_group, HEAD_SIZE)
    inverse = 1.0 / HEAD_SIZE**0.5
    scores = (
        jnp.einsum(
            "bkgd,btkd->bkgt", query_heads, gathered_keys, preferred_element_type=jnp.float32
        )
        * inverse
    )
    own_score = (
        jnp.einsum(
            "txvc,txc->txv",
            query_heads,
            new_token_key.reshape(local_rows, kv_local, HEAD_SIZE),
            preferred_element_type=jnp.float32,
        )
        * inverse
    )
    positions = jnp.arange(gathered_keys.shape[1], dtype=jnp.int32)
    live = (positions[None, :] < context_len[:, None])[:, None, None, :]
    scores = jnp.where(live, scores, jnp.float32(-1e30))
    top = jnp.maximum(jnp.max(scores, axis=-1), own_score)
    weights = jnp.where(live, jnp.exp(scores - top[..., None]), jnp.float32(0.0))
    own_weight = jnp.exp(own_score - top)
    total = jnp.sum(weights, axis=-1) + own_weight
    mixed = jnp.einsum(
        "bkgt,btkd->bkgd",
        weights.astype(jnp.bfloat16),
        gathered_values,
        preferred_element_type=jnp.float32,
    )
    fresh_wide = new_token_value.reshape(local_rows, kv_local, 1, HEAD_SIZE).astype(jnp.float32)
    mixed = mixed + rounded_values(own_weight)[..., None] * fresh_wide
    attention = (mixed / total[..., None]).reshape(local_rows, width_q).astype(jnp.bfloat16)
    out_rows = spread(attention, Z).reshape(z_size * local_rows, -1)
    sides = call(
        make_down_second(0),
        (t_size, z_size * local_rows // 2, 2 * rank),
        jnp.float32,
        column_slots,
        out_rows,
        z_rows,
        *out_pages,
    )
    term = call(
        make_up_second(local_width),
        (z_size * local_rows, output_up_weight.shape[2]),
        jnp.bfloat16,
        column_slots,
        exchange(sides, T),
        z_rows,
        *out_pages,
    )
    output_adapter_term = to_requests(term)
    return (attention, output_adapter_term.astype(jnp.bfloat16))


def solution(mesh):
    chips_y = 4
    wide, tensor = mesh.devices.shape
    devices = np.asarray(mesh.devices).reshape(chips_y, wide // chips_y, tensor)
    W = (Y, Z)
    return jax.shard_map(
        body,
        mesh=Mesh(devices, (Y, Z, T)),
        in_specs=(
            P(W, T),
            P(W, T),
            P(W, T),
            P(W, T),
            P(W, None, T),
            P(W, None, T),
            P(W, None),
            P(W),
            P(W),
            P(),
            P(W, T, None),
            P(W, None, T),
            P(W, None, T),
            P(W, None, T),
            P(W, T, None),
            P(W, None, T),
        ),
        out_specs=(P(W, T), P(W, T)),
        check_vma=False,
    )
```

```python
import jax
import jax.numpy as jnp
import numpy as np
from jax import lax
from jax.experimental import pallas as pl
from jax.experimental.pallas import tpu as pltpu
from jax.sharding import Mesh, PartitionSpec as P

HEAD_SIZE = 128
adapter_scale = 2.0
Y, Z, T = "y", "z", "tensor"


def rounded_values(values):
    return lax.optimization_barrier(values.astype(jnp.bfloat16)).astype(jnp.float32)


def exchange(blocks, axis):
    return lax.all_to_all(blocks, axis, 0, 0)


def spread(block, axis):
    copies = jnp.broadcast_to(block[None], (lax.axis_size(axis),) + block.shape)
    return exchange(copies, axis)


def summed(parts):
    return jnp.sum(parts.astype(jnp.float32), axis=0)


NT = (((1,), (1,)), ((), ()))
VMEM = pl.BlockSpec(memory_space=pltpu.VMEM)
SMEM = pl.BlockSpec(memory_space=pltpu.SMEM)


def call(kernel, shape, dtype, *operands, scalars=1):
    return pl.pallas_call(
        kernel,
        out_shape=jax.ShapeDtypeStruct(shape, dtype),
        in_specs=[SMEM] * scalars + [VMEM] * (len(operands) - scalars),
        out_specs=VMEM,
        compiler_params=pltpu.CompilerParams(vmem_limit_bytes=32 * 2**20),
    )(*operands)


def first_blocks(id_ref, slot_ref, hidden_ref, out_ref):
    rows, width = hidden_ref.shape
    tags = [
        jnp.full((1, 128), slot_ref[id_ref[r]].astype(jnp.float32), jnp.float32) for r in range(rows)
    ]
    block = jnp.concatenate(
        [hidden_ref[...], jnp.concatenate(tags, axis=0).astype(jnp.bfloat16)], axis=1
    )
    for z in range(out_ref.shape[0]):
        out_ref[z] = block


def second_blocks(from_z_ref, out_ref):
    rows = from_z_ref[...].reshape(out_ref.shape[1:])
    for y in range(out_ref.shape[0]):
        out_ref[y] = rows


def pack(*refs):
    out_ref, at = refs[-1], 0
    for ref in refs[:-1]:
        out_ref[:, :, at : at + ref.shape[2]] = ref[...]
        at += ref.shape[2]


def picked(slots_ref, tags, values, number):
    return jnp.where(tags == slots_ref[number].astype(jnp.float32), values, jnp.zeros_like(values))


def tags_of(rows_ref, at, width):
    return rows_ref[:, at : at + width].astype(jnp.float32)


def grown(slots_ref, tags, ranks, pages, at, width):
    count, rank, _ = pages.shape
    mine = [picked(slots_ref, tags, ranks, k) for k in range(count)]
    product = jnp.dot(
        jnp.concatenate(mine, axis=1).astype(jnp.bfloat16),
        pages[:, :, at : at + width].reshape(count * rank, width),
        preferred_element_type=jnp.float32,
    )
    return (adapter_scale * product).astype(jnp.bfloat16)


def make_up_first(cuts):
    def up_first(slots_ref, ranks_ref, rows_ref, pages, out_ref):
        rank = pages.shape[1]
        tags = tags_of(rows_ref, rows_ref.shape[1] - 128, rank)
        ranks = ranks_ref[...].astype(jnp.float32)
        for i in range(3):
            mine, width = ranks[:, i * rank : (i + 1) * rank], cuts[i + 1] - cuts[i]
            out_ref[:, cuts[i] : cuts[i + 1]] = grown(slots_ref, tags, mine, pages, cuts[i], width)

    return up_first


def down_second(slots_ref, out_rows_ref, rows_ref, pages, out_ref):
    count, rank, width = pages.shape
    rows = out_rows_ref[...]
    tags = tags_of(rows_ref, rows_ref.shape[1] - 128, rank)
    weights = pages[...].reshape(count * rank, width)
    product = lax.dot_general(rows, weights, NT, preferred_element_type=jnp.float32)
    total = jnp.zeros((rows.shape[0], rank), jnp.float32)
    for k in range(count):
        total = total + picked(slots_ref, tags, product[:, k * rank : (k + 1) * rank], k)
    half = rows.shape[0] // 2
    side = jnp.concatenate([total[:half], total[half:]], axis=1)
    for t in range(out_ref.shape[0]):
        out_ref[t] = side


def up_second(slots_ref, parts_ref, rows_ref, pages, out_ref):
    rank = pages.shape[1]
    side = jnp.sum(parts_ref[...], axis=0).astype(jnp.bfloat16).astype(jnp.float32)
    ranks = jnp.concatenate([side[:, :rank], side[:, rank:]], axis=0)
    tags = tags_of(rows_ref, rows_ref.shape[1] - 128, rank)
    out_ref[...] = grown(slots_ref, tags, ranks, pages, 0, out_ref.shape[1])


def to_requests(rows):
    return summed(exchange(rows.reshape(lax.axis_size(Z), -1, rows.shape[1]), Z))


def body(
    hidden,
    q_base,
    base_key,
    base_value,
    paged_key_cache,
    paged_value_cache,
    page_table,
    context_len,
    adapter_id,
    adapter_slot,
    query_key_value_down,
    query_up_weight,
    key_up_weight,
    value_up_weight,
    output_down_weight,
    output_up_weight,
):
    local_rows, local_width = hidden.shape
    local_count = query_key_value_down.shape[0]
    y_size, z_size, t_size = lax.axis_size(Y), lax.axis_size(Z), lax.axis_size(T)
    rank, width_q, width_k = query_up_weight.shape[1], q_base.shape[1], base_key.shape[1]
    cuts = (0, width_q, width_q + width_k, width_q + 2 * width_k)
    numbers = jnp.arange(local_count, dtype=jnp.int32)

    def slots_of(y):
        return (y * z_size + lax.axis_index(Z)) * local_count + numbers

    owned_slots = slots_of(lax.axis_index(Y))
    column_slots = slots_of(jnp.arange(y_size, dtype=jnp.int32)[:, None]).reshape(-1)
    up_shape = (local_count, rank, cuts[3])
    up_weights = call(
        pack, up_shape, jnp.bfloat16, query_up_weight, key_up_weight, value_up_weight, scalars=0
    )
    up_pages, down_pages, out_pages = [
        lax.all_gather(weight, Y, axis=0, tiled=True)
        for weight in (up_weights, jnp.swapaxes(output_down_weight, 1, 2), output_up_weight)
    ]
    z_blocks = call(
        first_blocks,
        (z_size, local_rows, local_width + 128),
        jnp.bfloat16,
        adapter_id,
        adapter_slot,
        hidden,
        scalars=2,
    )
    y_blocks = call(
        second_blocks,
        (y_size, z_size * local_rows, local_width + 128),
        jnp.bfloat16,
        exchange(z_blocks, Z),
        scalars=0,
    )
    z_rows = y_blocks[0]
    all_rows = exchange(y_blocks, Y).reshape(y_size * z_size * local_rows, -1)

    all_slots = all_rows[:, local_width].astype(jnp.int32)
    owned_mask = (all_slots[:, None] == owned_slots[None, :]).astype(jnp.float32)
    product = jnp.einsum(
        "nd,jdr->njr",
        all_rows[:, :local_width],
        query_key_value_down,
        preferred_element_type=jnp.float32,
    )
    part = jnp.sum(product * owned_mask[:, :, None], axis=1)
    share = z_size * local_rows // t_size
    shares = exchange(part.reshape(y_size * t_size, share, -1), (Y, T))
    ranks = spread(summed(shares).astype(jnp.bfloat16), T).reshape(z_size * local_rows, -1)
    delta = call(
        make_up_first(cuts),
        (z_size * local_rows, cuts[3]),
        jnp.bfloat16,
        column_slots,
        ranks,
        z_rows,
        up_pages,
    )
    adapter_delta = to_requests(delta)
    width_q = q_base.shape[1]
    width_k = base_key.shape[1]
    query_vector = (q_base.astype(jnp.float32) + adapter_delta[:, 0:width_q]).astype(jnp.bfloat16)
    new_token_key = (
        base_key.astype(jnp.float32) + adapter_delta[:, width_q : width_q + width_k]
    ).astype(jnp.bfloat16)
    new_token_value = (
        base_value.astype(jnp.float32) + adapter_delta[:, width_q + width_k : width_q + 2 * width_k]
    ).astype(jnp.bfloat16)
    kv_local = width_k // HEAD_SIZE
    head_group = width_q // width_k
    gathered_keys = paged_key_cache[page_table].reshape(local_rows, -1, kv_local, HEAD_SIZE)
    gathered_values = paged_value_cache[page_table].reshape(local_rows, -1, kv_local, HEAD_SIZE)
    query_heads = query_vector.reshape(local_rows, kv_local, head_group, HEAD_SIZE)
    inverse = 1.0 / HEAD_SIZE**0.5
    scores = (
        jnp.einsum(
            "bkgd,btkd->bkgt", query_heads, gathered_keys, preferred_element_type=jnp.float32
        )
        * inverse
    )
    own_score = (
        jnp.einsum(
            "txvc,txc->txv",
            query_heads,
            new_token_key.reshape(local_rows, kv_local, HEAD_SIZE),
            preferred_element_type=jnp.float32,
        )
        * inverse
    )
    positions = jnp.arange(gathered_keys.shape[1], dtype=jnp.int32)
    live = (positions[None, :] < context_len[:, None])[:, None, None, :]
    scores = jnp.where(live, scores, jnp.float32(-1e30))
    top = jnp.maximum(jnp.max(scores, axis=-1), own_score)
    weights = jnp.where(live, jnp.exp(scores - top[..., None]), jnp.float32(0.0))
    own_weight = jnp.exp(own_score - top)
    total = jnp.sum(weights, axis=-1) + own_weight
    mixed = jnp.einsum(
        "bkgt,btkd->bkgd",
        weights.astype(jnp.bfloat16),
        gathered_values,
        preferred_element_type=jnp.float32,
    )
    fresh_wide = new_token_value.reshape(local_rows, kv_local, 1, HEAD_SIZE).astype(jnp.float32)
    mixed = mixed + rounded_values(own_weight)[..., None] * fresh_wide
    attention = (mixed / total[..., None]).reshape(local_rows, width_q).astype(jnp.bfloat16)
    out_rows = spread(attention, Z).reshape(z_size * local_rows, -1)
    sides = call(
        down_second,
        (t_size, z_size * local_rows // 2, 2 * rank),
        jnp.float32,
        column_slots,
        out_rows,
        z_rows,
        down_pages,
    )
    term = call(
        up_second,
        (z_size * local_rows, output_up_weight.shape[2]),
        jnp.bfloat16,
        column_slots,
        exchange(sides, T),
        z_rows,
        out_pages,
    )
    output_adapter_term = to_requests(term)
    return (attention, output_adapter_term.astype(jnp.bfloat16))


def solution(mesh):
    chips_y = 4
    wide, tensor = mesh.devices.shape
    devices = np.asarray(mesh.devices).reshape(chips_y, wide // chips_y, tensor)
    W = (Y, Z)
    return jax.shard_map(
        body,
        mesh=Mesh(devices, (Y, Z, T)),
        in_specs=(
            P(W, T),
            P(W, T),
            P(W, T),
            P(W, T),
            P(W, None, T),
            P(W, None, T),
            P(W, None),
            P(W),
            P(W),
            P(),
            P(W, T, None),
            P(W, None, T),
            P(W, None, T),
            P(W, None, T),
            P(W, T, None),
            P(W, None, T),
        ),
        out_specs=(P(W, T), P(W, T)),
        check_vma=False,
    )
```

```python
import jax
import jax.numpy as jnp
import numpy as np
from jax import lax
from jax.experimental import pallas as pl
from jax.experimental.pallas import tpu as pltpu
from jax.sharding import Mesh, PartitionSpec as P

adapter_scale = 2.0
Y, Z, T = "y", "z", "tensor"


def exchange(blocks, axis):
    return lax.all_to_all(blocks, axis, 0, 0)


def spread(block, axis):
    copies = jnp.broadcast_to(block[None], (lax.axis_size(axis),) + block.shape)
    return exchange(copies, axis)


def summed(parts):
    return jnp.sum(parts.astype(jnp.float32), axis=0)


NT = (((1,), (1,)), ((), ()))
VMEM = pl.BlockSpec(memory_space=pltpu.VMEM)
SMEM = pl.BlockSpec(memory_space=pltpu.SMEM)


ANY = pl.BlockSpec(memory_space=pl.ANY)


def call(kernel, shape, dtype, *operands, scalars=1, after=()):
    count = len(operands)

    def run(*refs):
        kernel(*refs[:count], *refs[count + len(after) :])

    return pl.pallas_call(
        run,
        out_shape=jax.ShapeDtypeStruct(shape, dtype),
        in_specs=[SMEM] * scalars + [VMEM] * (count - scalars) + [ANY] * len(after),
        out_specs=VMEM,
        compiler_params=pltpu.CompilerParams(vmem_limit_bytes=32 * 2**20),
    )(*operands, *after)


def first_blocks(id_hbm, slot_hbm, hidden_hbm, out_ref, id_ref, slot_ref, hidden_ref, sems):
    copies = [
        pltpu.make_async_copy(source, target, sems.at[i])
        for i, (source, target) in enumerate(
            ((id_hbm, id_ref), (slot_hbm, slot_ref), (hidden_hbm, hidden_ref))
        )
    ]
    for copy in copies:
        copy.start()
    for copy in copies:
        copy.wait()
    rows, width = hidden_ref.shape
    tags = [
        jnp.full((1, 128), slot_ref[id_ref[r]].astype(jnp.float32), jnp.float32) for r in range(rows)
    ]
    block = jnp.concatenate(
        [hidden_ref[...], jnp.concatenate(tags, axis=0).astype(jnp.bfloat16)], axis=1
    )
    for z in range(out_ref.shape[0]):
        out_ref[z] = block


def attend(
    table_ref, length_ref, terms_ref, q_ref, k_ref, v_ref, keys_ref, values_ref, out_ref, block_ref
):
    rows, width_q = q_ref.shape
    size = k_ref.shape[1]
    heads = width_q // size
    delta = summed(terms_ref[...])
    parts = (
        q_ref[...].astype(jnp.float32) + delta[:, :width_q],
        k_ref[...].astype(jnp.float32) + delta[:, width_q : width_q + size],
        v_ref[...].astype(jnp.float32) + delta[:, width_q + size :],
    )
    query, key, value = [part.astype(jnp.bfloat16).astype(jnp.float32) for part in parts]
    inverse = 1.0 / size**0.5
    done = []
    for r in range(rows):
        pages = [table_ref[r, i] for i in range(table_ref.shape[1])]
        q = jnp.concatenate(
            [query[r : r + 1, h * size : (h + 1) * size] for h in range(heads)], axis=0
        )
        keys = jnp.concatenate([keys_ref[page] for page in pages], axis=0)
        scores = lax.dot_general(
            q.astype(jnp.bfloat16), keys, NT, preferred_element_type=jnp.float32
        )
        live = lax.broadcasted_iota(jnp.int32, scores.shape, 1) < length_ref[r]
        scores = jnp.where(live, scores * inverse, jnp.float32(-1e30))
        own = jnp.sum(q * key[r : r + 1], axis=1, keepdims=True) * inverse
        top = jnp.maximum(jnp.max(scores, axis=1, keepdims=True), own)
        weights = jnp.where(live, jnp.exp(scores - top), 0.0)
        own_weight = jnp.exp(own - top)
        total = jnp.sum(weights, axis=1, keepdims=True) + own_weight
        values = jnp.concatenate([values_ref[page] for page in pages], axis=0)
        mixed = jnp.dot(weights.astype(jnp.bfloat16), values, preferred_element_type=jnp.float32)
        own_rounded = own_weight.astype(jnp.bfloat16).astype(jnp.float32)
        mixed = (mixed + own_rounded * value[r : r + 1]) / total
        done.append(jnp.concatenate([mixed[h : h + 1] for h in range(heads)], axis=1))
    attention = jnp.concatenate(done, axis=0).astype(jnp.bfloat16)
    out_ref[...] = attention
    for z in range(block_ref.shape[0]):
        block_ref[z] = attention


def second_blocks(from_z_ref, out_ref):
    rows = from_z_ref[...].reshape(out_ref.shape[1:])
    for y in range(out_ref.shape[0]):
        out_ref[y] = rows


def pack(*refs):
    out_ref, at = refs[-1], 0
    for ref in refs[:-1]:
        out_ref[:, :, at : at + ref.shape[2]] = ref[...]
        at += ref.shape[2]


def picked(slots_ref, tags, values, number):
    return jnp.where(tags == slots_ref[number].astype(jnp.float32), values, jnp.zeros_like(values))


def down_first(slots_ref, rows_ref, weight_ref, out_ref):
    width = weight_ref.shape[2]
    rows, tags = rows_ref[:, :width], rows_ref[:, width : width + 1].astype(jnp.float32)
    total = None
    for j in range(weight_ref.shape[0]):
        product = lax.dot_general(rows, weight_ref[j], NT, preferred_element_type=jnp.float32)
        mine = picked(slots_ref, tags, product, j)
        total = mine if total is None else total + mine
    out_ref[...] = total


def tags_of(rows_ref, at, width):
    return rows_ref[:, at : at + width].astype(jnp.float32)


def grown(slots_ref, tags, ranks, pages, at, width):
    total = None
    for k, page in enumerate(pages):
        count, rank, _ = page.shape
        mine = [picked(slots_ref, tags, ranks, k * count + j) for j in range(count)]
        product = jnp.dot(
            jnp.concatenate(mine, axis=1).astype(jnp.bfloat16),
            page[:, :, at : at + width].reshape(count * rank, width),
            preferred_element_type=jnp.float32,
        )
        total = product if total is None else total + product
    return (adapter_scale * total).astype(jnp.bfloat16)


def make_up_first(cuts):
    def up_first(slots_ref, ranks_ref, rows_ref, *refs):
        pages, out_ref = refs[:-1], refs[-1]
        rank = pages[0].shape[1]
        tags = tags_of(rows_ref, rows_ref.shape[1] - 128, rank)
        ranks = ranks_ref[...].astype(jnp.float32)
        for i in range(3):
            out_ref[:, cuts[i] : cuts[i + 1]] = grown(
                slots_ref,
                tags,
                ranks[:, i * rank : (i + 1) * rank],
                pages,
                cuts[i],
                cuts[i + 1] - cuts[i],
            )

    return up_first


def make_down_second(at):
    def down_second(slots_ref, out_rows_ref, rows_ref, *refs):
        pages, out_ref = refs[:-1], refs[-1]
        count, rank, _ = pages[0].shape
        rows = out_rows_ref[...]
        tags = tags_of(rows_ref, rows_ref.shape[1] - 128, rank)
        total = jnp.zeros((rows.shape[0], rank), jnp.float32)
        for k, page in enumerate(pages):
            for j in range(count):
                weight = page[j, :, at : at + rows.shape[1]]
                product = lax.dot_general(rows, weight, NT, preferred_element_type=jnp.float32)
                total = total + picked(slots_ref, tags, product, k * count + j)
        half = rows.shape[0] // 2
        side = jnp.concatenate([total[:half], total[half:]], axis=1)
        for t in range(out_ref.shape[0]):
            out_ref[t] = side

    return down_second


def make_up_second(at):
    def up_second(slots_ref, parts_ref, rows_ref, *refs):
        pages, out_ref = refs[:-1], refs[-1]
        rank = pages[0].shape[1]
        side = jnp.sum(parts_ref[...], axis=0).astype(jnp.bfloat16).astype(jnp.float32)
        ranks = jnp.concatenate([side[:, :rank], side[:, rank:]], axis=0)
        tags = tags_of(rows_ref, rows_ref.shape[1] - 128, rank)
        out_ref[...] = grown(slots_ref, tags, ranks, pages, at, out_ref.shape[1])

    return up_second


def to_requests(rows):
    return summed(exchange(rows.reshape(lax.axis_size(Z), -1, rows.shape[1]), Z))


def body(
    hidden,
    q_base,
    base_key,
    base_value,
    paged_key_cache,
    paged_value_cache,
    page_table,
    context_len,
    adapter_id,
    adapter_slot,
    query_key_value_down,
    query_up_weight,
    key_up_weight,
    value_up_weight,
    output_down_weight,
    output_up_weight,
):
    local_rows, local_width = hidden.shape
    local_count = query_key_value_down.shape[0]
    y_size, z_size, t_size = lax.axis_size(Y), lax.axis_size(Z), lax.axis_size(T)
    rank, width_q, width_k = query_up_weight.shape[1], q_base.shape[1], base_key.shape[1]
    cuts = (0, width_q, width_q + width_k, width_q + 2 * width_k)
    own_y = lax.axis_index(Y)
    places = jnp.arange(y_size, dtype=jnp.int32)
    numbers = jnp.arange(local_count, dtype=jnp.int32)
    column_slots = (
        ((own_y - places[:, None]) % y_size * z_size + lax.axis_index(Z)) * local_count + numbers
    ).reshape(-1)

    def packed(*weights, after=()):
        width = sum(weight.shape[2] for weight in weights)
        shape = (local_count, rank, width)
        mine = call(pack, shape, jnp.bfloat16, *weights, scalars=0, after=after)
        return [mine] + [
            lax.ppermute(mine, Y, [(i, (i + k) % y_size) for i in range(y_size)])
            for k in range(1, y_size)
        ]

    up_pages = packed(query_up_weight, key_up_weight, value_up_weight)
    z_blocks = pl.pallas_call(
        first_blocks,
        out_shape=jax.ShapeDtypeStruct((z_size, local_rows, local_width + 128), jnp.bfloat16),
        in_specs=[ANY] * 3,
        out_specs=VMEM,
        scratch_shapes=[
            pltpu.SMEM(adapter_id.shape, jnp.int32),
            pltpu.SMEM(adapter_slot.shape, jnp.int32),
            pltpu.VMEM(hidden.shape, jnp.bfloat16),
            pltpu.SemaphoreType.DMA((3,)),
        ],
    )(adapter_id, adapter_slot, hidden)
    y_blocks = call(
        second_blocks,
        (y_size, z_size * local_rows, local_width + 128),
        jnp.bfloat16,
        exchange(z_blocks, Z),
        scalars=0,
        after=up_pages[1:2],
    )
    z_rows = y_blocks[0]
    all_rows = exchange(y_blocks, Y).reshape(y_size * z_size * local_rows, -1)

    part = call(
        down_first,
        (y_size * z_size * local_rows, query_key_value_down.shape[2]),
        jnp.float32,
        column_slots,
        all_rows,
        jnp.swapaxes(query_key_value_down, 1, 2),
        after=up_pages[2:],
    )
    share = z_size * local_rows // t_size
    shares = exchange(part.reshape(y_size * t_size, share, -1), (Y, T))
    ranks = spread(summed(shares).astype(jnp.bfloat16), T).reshape(z_size * local_rows, -1)
    delta = call(
        make_up_first(cuts),
        (z_size * local_rows, cuts[3]),
        jnp.bfloat16,
        column_slots,
        ranks,
        z_rows,
        *up_pages,
    )
    out_pages = packed(
        jnp.swapaxes(output_down_weight, 1, 2), output_up_weight, after=(shares,)
    )
    terms = exchange(delta.reshape(z_size, local_rows, cuts[3]), Z)
    attention, out_blocks = pl.pallas_call(
        attend,
        out_shape=[
            jax.ShapeDtypeStruct(q_base.shape, jnp.bfloat16),
            jax.ShapeDtypeStruct((z_size,) + q_base.shape, jnp.bfloat16),
        ],
        in_specs=[SMEM] * 2 + [VMEM] * 6,
        out_specs=[VMEM] * 2,
        compiler_params=pltpu.CompilerParams(vmem_limit_bytes=32 * 2**20),
    )(
        page_table,
        context_len,
        terms,
        q_base,
        base_key,
        base_value,
        paged_key_cache,
        paged_value_cache,
    )
    out_rows = exchange(out_blocks, Z).reshape(z_size * local_rows, -1)
    sides = call(
        make_down_second(0),
        (t_size, z_size * local_rows // 2, 2 * rank),
        jnp.float32,
        column_slots,
        out_rows,
        z_rows,
        *out_pages,
    )
    term = call(
        make_up_second(local_width),
        (z_size * local_rows, output_up_weight.shape[2]),
        jnp.bfloat16,
        column_slots,
        exchange(sides, T),
        z_rows,
        *out_pages,
    )
    output_adapter_term = to_requests(term)
    return (attention, output_adapter_term.astype(jnp.bfloat16))


def solution(mesh):
    chips_y = 4
    wide, tensor = mesh.devices.shape
    devices = np.asarray(mesh.devices).reshape(chips_y, wide // chips_y, tensor)
    W = (Y, Z)
    return jax.shard_map(
        body,
        mesh=Mesh(devices, (Y, Z, T)),
        in_specs=(
            P(W, T),
            P(W, T),
            P(W, T),
            P(W, T),
            P(W, None, T),
            P(W, None, T),
            P(W, None),
            P(W),
            P(W),
            P(),
            P(W, T, None),
            P(W, None, T),
            P(W, None, T),
            P(W, None, T),
            P(W, T, None),
            P(W, None, T),
        ),
        out_specs=(P(W, T), P(W, T)),
        check_vma=False,
    )
```

```python
import jax
import jax.numpy as jnp
import numpy as np
from jax import lax
from jax.experimental import pallas as pl
from jax.experimental.pallas import tpu as pltpu
from jax.sharding import Mesh, PartitionSpec as P

adapter_scale = 2.0
Y, Z, T = "y", "z", "tensor"


def exchange(blocks, axis):
    return lax.all_to_all(blocks, axis, 0, 0)


def spread(block, axis):
    copies = jnp.broadcast_to(block[None], (lax.axis_size(axis),) + block.shape)
    return exchange(copies, axis)


def summed(parts):
    return jnp.sum(parts.astype(jnp.float32), axis=0)


NT = (((1,), (1,)), ((), ()))
VMEM = pl.BlockSpec(memory_space=pltpu.VMEM)
SMEM = pl.BlockSpec(memory_space=pltpu.SMEM)


ANY = pl.BlockSpec(memory_space=pl.ANY)


def call(kernel, shape, dtype, *operands, scalars=1, after=()):
    count = len(operands)

    def run(*refs):
        kernel(*refs[:count], *refs[count + len(after) :])

    return pl.pallas_call(
        run,
        out_shape=jax.ShapeDtypeStruct(shape, dtype),
        in_specs=[SMEM] * scalars + [VMEM] * (count - scalars) + [ANY] * len(after),
        out_specs=VMEM,
        compiler_params=pltpu.CompilerParams(vmem_limit_bytes=32 * 2**20),
    )(*operands, *after)


def fetch(sources, targets, sems):
    copies = [
        pltpu.make_async_copy(source, target, sems.at[i])
        for i, (source, target) in enumerate(zip(sources, targets))
    ]
    for copy in copies:
        copy.start()
    return copies


def first_blocks(id_hbm, slot_hbm, hidden_hbm, out_ref, id_ref, slot_ref, hidden_ref, sems):
    for copy in fetch((id_hbm, slot_hbm, hidden_hbm), (id_ref, slot_ref, hidden_ref), sems):
        copy.wait()
    rows, width = hidden_ref.shape
    tags = [
        jnp.full((1, 128), slot_ref[id_ref[r]].astype(jnp.float32), jnp.float32) for r in range(rows)
    ]
    block = jnp.concatenate(
        [hidden_ref[...], jnp.concatenate(tags, axis=0).astype(jnp.bfloat16)], axis=1
    )
    for z in range(out_ref.shape[0]):
        out_ref[z] = block


def attend(*refs):
    sources, (out_ref, block_ref), held, sems = refs[:8], refs[8:10], refs[10:18], refs[18]
    table_ref, length_ref, terms_ref, q_ref, k_ref, v_ref, keys_ref, values_ref = held
    for copy in fetch(sources, held, sems):
        copy.wait()
    rows, width_q = q_ref.shape
    size = k_ref.shape[1]
    heads = width_q // size
    delta = summed(terms_ref[...])
    parts = (
        q_ref[...].astype(jnp.float32) + delta[:, :width_q],
        k_ref[...].astype(jnp.float32) + delta[:, width_q : width_q + size],
        v_ref[...].astype(jnp.float32) + delta[:, width_q + size :],
    )
    query, key, value = [part.astype(jnp.bfloat16).astype(jnp.float32) for part in parts]
    inverse = 1.0 / size**0.5
    done = []
    for r in range(rows):
        pages = [table_ref[r, i] for i in range(table_ref.shape[1])]
        q = jnp.concatenate(
            [query[r : r + 1, h * size : (h + 1) * size] for h in range(heads)], axis=0
        )
        keys = jnp.concatenate([keys_ref[page] for page in pages], axis=0)
        scores = lax.dot_general(
            q.astype(jnp.bfloat16), keys, NT, preferred_element_type=jnp.float32
        )
        live = lax.broadcasted_iota(jnp.int32, scores.shape, 1) < length_ref[r]
        scores = jnp.where(live, scores * inverse, jnp.float32(-1e30))
        own = jnp.sum(q * key[r : r + 1], axis=1, keepdims=True) * inverse
        top = jnp.maximum(jnp.max(scores, axis=1, keepdims=True), own)
        weights = jnp.where(live, jnp.exp(scores - top), 0.0)
        own_weight = jnp.exp(own - top)
        total = jnp.sum(weights, axis=1, keepdims=True) + own_weight
        values = jnp.concatenate([values_ref[page] for page in pages], axis=0)
        mixed = jnp.dot(weights.astype(jnp.bfloat16), values, preferred_element_type=jnp.float32)
        own_rounded = own_weight.astype(jnp.bfloat16).astype(jnp.float32)
        mixed = (mixed + own_rounded * value[r : r + 1]) / total
        done.append(jnp.concatenate([mixed[h : h + 1] for h in range(heads)], axis=1))
    attention = jnp.concatenate(done, axis=0).astype(jnp.bfloat16)
    out_ref[...] = attention
    for z in range(block_ref.shape[0]):
        block_ref[z] = attention


def second_blocks(from_z_ref, out_ref):
    rows = from_z_ref[...].reshape(out_ref.shape[1:])
    for y in range(out_ref.shape[0]):
        out_ref[y] = rows


def pack(*refs):
    out_ref, at = refs[-1], 0
    for ref in refs[:-1]:
        out_ref[:, :, at : at + ref.shape[2]] = ref[...]
        at += ref.shape[2]


def picked(slots_ref, tags, values, number):
    return jnp.where(tags == slots_ref[number].astype(jnp.float32), values, jnp.zeros_like(values))


def down_first(slots_ref, rows_ref, weight_ref, out_ref):
    width = weight_ref.shape[2]
    rows, tags = rows_ref[:, :width], rows_ref[:, width : width + 1].astype(jnp.float32)
    total = None
    for j in range(weight_ref.shape[0]):
        product = lax.dot_general(rows, weight_ref[j], NT, preferred_element_type=jnp.float32)
        mine = picked(slots_ref, tags, product, j)
        total = mine if total is None else total + mine
    out_ref[...] = total


def tags_of(rows_ref, at, width):
    return rows_ref[:, at : at + width].astype(jnp.float32)


def grown(slots_ref, tags, ranks, pages, at, width):
    total = None
    for k, page in enumerate(pages):
        count, rank, _ = page.shape
        mine = [picked(slots_ref, tags, ranks, k * count + j) for j in range(count)]
        product = jnp.dot(
            jnp.concatenate(mine, axis=1).astype(jnp.bfloat16),
            page[:, :, at : at + width].reshape(count * rank, width),
            preferred_element_type=jnp.float32,
        )
        total = product if total is None else total + product
    return (adapter_scale * total).astype(jnp.bfloat16)


def up_first(slots_ref, ranks_ref, rows_ref, q_up, k_up, v_up, out_ref):
    rank = q_up.shape[1]
    tags = tags_of(rows_ref, rows_ref.shape[1] - 128, rank)
    ranks = ranks_ref[...].astype(jnp.float32)
    at = 0
    for i, page in enumerate((q_up, k_up, v_up)):
        width = page.shape[2]
        mine = ranks[:, i * rank : (i + 1) * rank]
        out_ref[:, at : at + width] = grown(slots_ref, tags, mine, [page], 0, width)
        at += width


def term_blocks(from_y_ref, out_ref):
    out_ref[...] = summed(from_y_ref[...]).reshape(out_ref.shape).astype(jnp.bfloat16)


def make_down_second(at):
    def down_second(slots_ref, out_rows_ref, rows_ref, *refs):
        pages, out_ref = refs[:-1], refs[-1]
        count, rank, _ = pages[0].shape
        rows = out_rows_ref[...]
        tags = tags_of(rows_ref, rows_ref.shape[1] - 128, rank)
        total = jnp.zeros((rows.shape[0], rank), jnp.float32)
        for k, page in enumerate(pages):
            for j in range(count):
                weight = page[j, :, at : at + rows.shape[1]]
                product = lax.dot_general(rows, weight, NT, preferred_element_type=jnp.float32)
                total = total + picked(slots_ref, tags, product, k * count + j)
        half = rows.shape[0] // 2
        side = jnp.concatenate([total[:half], total[half:]], axis=1)
        for t in range(out_ref.shape[0]):
            out_ref[t] = side

    return down_second


def make_up_second(at):
    def up_second(slots_ref, parts_ref, rows_ref, *refs):
        pages, out_ref = refs[:-1], refs[-1]
        rank = pages[0].shape[1]
        side = jnp.sum(parts_ref[...], axis=0).astype(jnp.bfloat16).astype(jnp.float32)
        ranks = jnp.concatenate([side[:, :rank], side[:, rank:]], axis=0)
        tags = tags_of(rows_ref, rows_ref.shape[1] - 128, rank)
        out_ref[...] = grown(slots_ref, tags, ranks, pages, at, out_ref.shape[1])

    return up_second


def to_requests(rows):
    return summed(exchange(rows.reshape(lax.axis_size(Z), -1, rows.shape[1]), Z))


def body(
    hidden,
    q_base,
    base_key,
    base_value,
    paged_key_cache,
    paged_value_cache,
    page_table,
    context_len,
    adapter_id,
    adapter_slot,
    query_key_value_down,
    query_up_weight,
    key_up_weight,
    value_up_weight,
    output_down_weight,
    output_up_weight,
):
    local_rows, local_width = hidden.shape
    local_count = query_key_value_down.shape[0]
    y_size, z_size, t_size = lax.axis_size(Y), lax.axis_size(Z), lax.axis_size(T)
    rank, width_q, width_k = query_up_weight.shape[1], q_base.shape[1], base_key.shape[1]
    cuts = (0, width_q, width_q + width_k, width_q + 2 * width_k)
    own_y = lax.axis_index(Y)
    places = jnp.arange(y_size, dtype=jnp.int32)
    numbers = jnp.arange(local_count, dtype=jnp.int32)
    column_slots = (
        ((own_y - places[:, None]) % y_size * z_size + lax.axis_index(Z)) * local_count + numbers
    ).reshape(-1)

    def packed(*weights, after=()):
        width = sum(weight.shape[2] for weight in weights)
        shape = (local_count, rank, width)
        mine = call(pack, shape, jnp.bfloat16, *weights, scalars=0, after=after)
        return [mine] + [
            lax.ppermute(mine, Y, [(i, (i + k) % y_size) for i in range(y_size)])
            for k in range(1, y_size)
        ]

    z_blocks = pl.pallas_call(
        first_blocks,
        out_shape=jax.ShapeDtypeStruct((z_size, local_rows, local_width + 128), jnp.bfloat16),
        in_specs=[ANY] * 3,
        out_specs=VMEM,
        scratch_shapes=[
            pltpu.SMEM(adapter_id.shape, jnp.int32),
            pltpu.SMEM(adapter_slot.shape, jnp.int32),
            pltpu.VMEM(hidden.shape, jnp.bfloat16),
            pltpu.SemaphoreType.DMA((3,)),
        ],
    )(adapter_id, adapter_slot, hidden)
    y_blocks = call(
        second_blocks,
        (y_size, z_size * local_rows, local_width + 128),
        jnp.bfloat16,
        exchange(z_blocks, Z),
        scalars=0,
    )
    z_rows = y_blocks[0]
    all_rows = exchange(y_blocks, Y).reshape(y_size * z_size * local_rows, -1)

    part = call(
        down_first,
        (y_size * z_size * local_rows, query_key_value_down.shape[2]),
        jnp.float32,
        column_slots,
        all_rows,
        jnp.swapaxes(query_key_value_down, 1, 2),
    )
    shares = exchange(part.reshape(t_size, -1, part.shape[1]), T)
    ranks = spread(summed(shares).astype(jnp.bfloat16), T).reshape(part.shape)
    delta = call(
        up_first,
        (all_rows.shape[0], cuts[3]),
        jnp.bfloat16,
        column_slots,
        ranks,
        all_rows,
        query_up_weight,
        key_up_weight,
        value_up_weight,
    )
    from_y = exchange(delta.reshape(y_size, z_size * local_rows, cuts[3]), Y)
    terms = exchange(
        call(term_blocks, (z_size, local_rows, cuts[3]), jnp.bfloat16, from_y, scalars=0), Z
    )
    out_pages = packed(
        jnp.swapaxes(output_down_weight, 1, 2), output_up_weight, after=(from_y,)
    )
    attention, out_blocks = pl.pallas_call(
        attend,
        out_shape=[
            jax.ShapeDtypeStruct(q_base.shape, jnp.bfloat16),
            jax.ShapeDtypeStruct((z_size,) + q_base.shape, jnp.bfloat16),
        ],
        in_specs=[ANY] * 8,
        out_specs=[VMEM] * 2,
        scratch_shapes=[
            pltpu.SMEM(page_table.shape, jnp.int32),
            pltpu.SMEM(context_len.shape, jnp.int32),
            pltpu.VMEM(terms.shape, jnp.bfloat16),
            pltpu.VMEM(q_base.shape, jnp.bfloat16),
            pltpu.VMEM(base_key.shape, jnp.bfloat16),
            pltpu.VMEM(base_value.shape, jnp.bfloat16),
            pltpu.VMEM(paged_key_cache.shape, jnp.bfloat16),
            pltpu.VMEM(paged_value_cache.shape, jnp.bfloat16),
            pltpu.SemaphoreType.DMA((8,)),
        ],
        compiler_params=pltpu.CompilerParams(vmem_limit_bytes=32 * 2**20),
    )(
        page_table,
        context_len,
        terms,
        q_base,
        base_key,
        base_value,
        paged_key_cache,
        paged_value_cache,
    )
    out_rows = exchange(out_blocks, Z).reshape(z_size * local_rows, -1)
    sides = call(
        make_down_second(0),
        (t_size, z_size * local_rows // 2, 2 * rank),
        jnp.float32,
        column_slots,
        out_rows,
        z_rows,
        *out_pages,
    )
    term = call(
        make_up_second(local_width),
        (z_size * local_rows, output_up_weight.shape[2]),
        jnp.bfloat16,
        column_slots,
        exchange(sides, T),
        z_rows,
        *out_pages,
    )
    output_adapter_term = to_requests(term)
    return (attention, output_adapter_term.astype(jnp.bfloat16))


def solution(mesh):
    chips_y = 4
    wide, tensor = mesh.devices.shape
    devices = np.asarray(mesh.devices).reshape(chips_y, wide // chips_y, tensor)
    W = (Y, Z)
    return jax.shard_map(
        body,
        mesh=Mesh(devices, (Y, Z, T)),
        in_specs=(
            P(W, T),
            P(W, T),
            P(W, T),
            P(W, T),
            P(W, None, T),
            P(W, None, T),
            P(W, None),
            P(W),
            P(W),
            P(),
            P(W, T, None),
            P(W, None, T),
            P(W, None, T),
            P(W, None, T),
            P(W, T, None),
            P(W, None, T),
        ),
        out_specs=(P(W, T), P(W, T)),
        check_vma=False,
    )
```

```python
import jax
import jax.numpy as jnp
import numpy as np
from jax import lax
from jax.experimental import pallas as pl
from jax.experimental.pallas import tpu as pltpu
from jax.sharding import Mesh, PartitionSpec as P

adapter_scale = 2.0
Y, Z, T = "y", "z", "tensor"


def exchange(blocks, axis):
    return lax.all_to_all(blocks, axis, 0, 0)


def spread(block, axis):
    copies = jnp.broadcast_to(block[None], (lax.axis_size(axis),) + block.shape)
    return exchange(copies, axis)


def summed(parts):
    return jnp.sum(parts.astype(jnp.float32), axis=0)


NT = (((1,), (1,)), ((), ()))
VMEM = pl.BlockSpec(memory_space=pltpu.VMEM)
SMEM = pl.BlockSpec(memory_space=pltpu.SMEM)


ANY = pl.BlockSpec(memory_space=pl.ANY)


def call(kernel, shape, dtype, *operands, scalars=1, after=()):
    count = len(operands)

    def run(*refs):
        kernel(*refs[:count], *refs[count + len(after) :])

    return pl.pallas_call(
        run,
        out_shape=jax.ShapeDtypeStruct(shape, dtype),
        in_specs=[SMEM] * scalars + [VMEM] * (count - scalars) + [ANY] * len(after),
        out_specs=VMEM,
        compiler_params=pltpu.CompilerParams(vmem_limit_bytes=32 * 2**20),
    )(*operands, *after)


def fetch(sources, targets, sems):
    copies = [
        pltpu.make_async_copy(source, target, sems.at[i])
        for i, (source, target) in enumerate(zip(sources, targets))
    ]
    for copy in copies:
        copy.start()
    return copies


def first_blocks(id_hbm, slot_hbm, hidden_hbm, out_ref, id_ref, slot_ref, hidden_ref, sems):
    for copy in fetch((id_hbm, slot_hbm, hidden_hbm), (id_ref, slot_ref, hidden_ref), sems):
        copy.wait()
    rows, width = hidden_ref.shape
    tags = [
        jnp.full((1, 128), slot_ref[id_ref[r]].astype(jnp.float32), jnp.float32) for r in range(rows)
    ]
    block = jnp.concatenate(
        [hidden_ref[...], jnp.concatenate(tags, axis=0).astype(jnp.bfloat16)], axis=1
    )
    for z in range(out_ref.shape[0]):
        out_ref[z] = block


def attend(*refs):
    sources, (out_ref, block_ref), held, sems = refs[:8], refs[8:10], refs[10:18], refs[18]
    table_ref, length_ref, terms_ref, q_ref, k_ref, v_ref, keys_ref, values_ref = held
    copies = fetch(sources, held, sems)
    for copy in copies[:7]:
        copy.wait()
    rows, width_q = q_ref.shape
    size = k_ref.shape[1]
    heads = width_q // size
    delta = summed(terms_ref[...])
    parts = (
        q_ref[...].astype(jnp.float32) + delta[:, :width_q],
        k_ref[...].astype(jnp.float32) + delta[:, width_q : width_q + size],
        v_ref[...].astype(jnp.float32) + delta[:, width_q + size :],
    )
    query, key, value = [part.astype(jnp.bfloat16).astype(jnp.float32) for part in parts]
    inverse = 1.0 / size**0.5
    done = []
    for r in range(rows):
        pages = [table_ref[r, i] for i in range(table_ref.shape[1])]
        q = jnp.concatenate(
            [query[r : r + 1, h * size : (h + 1) * size] for h in range(heads)], axis=0
        )
        keys = jnp.concatenate([keys_ref[page] for page in pages], axis=0)
        scores = lax.dot_general(
            q.astype(jnp.bfloat16), keys, NT, preferred_element_type=jnp.float32
        )
        live = lax.broadcasted_iota(jnp.int32, scores.shape, 1) < length_ref[r]
        scores = jnp.where(live, scores * inverse, jnp.float32(-1e30))
        own = jnp.sum(q * key[r : r + 1], axis=1, keepdims=True) * inverse
        top = jnp.maximum(jnp.max(scores, axis=1, keepdims=True), own)
        weights = jnp.where(live, jnp.exp(scores - top), 0.0)
        own_weight = jnp.exp(own - top)
        total = jnp.sum(weights, axis=1, keepdims=True) + own_weight
        if r == 0:
            copies[7].wait()
        values = jnp.concatenate([values_ref[page] for page in pages], axis=0)
        mixed = jnp.dot(weights.astype(jnp.bfloat16), values, preferred_element_type=jnp.float32)
        own_rounded = own_weight.astype(jnp.bfloat16).astype(jnp.float32)
        mixed = (mixed + own_rounded * value[r : r + 1]) / total
        done.append(jnp.concatenate([mixed[h : h + 1] for h in range(heads)], axis=1))
    attention = jnp.concatenate(done, axis=0).astype(jnp.bfloat16)
    out_ref[...] = attention
    for z in range(block_ref.shape[0]):
        block_ref[z] = attention


def second_blocks(from_z_ref, out_ref):
    rows = from_z_ref[...].reshape(out_ref.shape[1:])
    for y in range(out_ref.shape[0]):
        out_ref[y] = rows


def pack(*refs):
    out_ref, at = refs[-1], 0
    for ref in refs[:-1]:
        out_ref[:, :, at : at + ref.shape[2]] = ref[...]
        at += ref.shape[2]


def picked(slots_ref, tags, values, number):
    return jnp.where(tags == slots_ref[number].astype(jnp.float32), values, jnp.zeros_like(values))


def write_packed(ranks, out_ref):
    shares, packed_rows, lanes = out_ref.shape
    rows = ranks.shape[0] // shares
    half = packed_rows - rows
    for t in range(shares):
        share = ranks[t * rows : (t + 1) * rows]
        out_ref[t, :rows] = share[:, :lanes]
        out_ref[t, rows:] = jnp.concatenate(
            [share[:half, lanes:], share[half:, lanes:]], axis=1
        )


def read_packed(ref):
    shares, packed_rows, lanes = ref.shape
    rows = packed_rows * 2 // 3
    first, last = [], []
    for t in range(shares):
        share = ref[t].astype(jnp.float32)
        first.append(share[:rows])
        last += [share[rows:, : lanes // 2], share[rows:, lanes // 2 :]]
    return jnp.concatenate([jnp.concatenate(first, 0), jnp.concatenate(last, 0)], axis=1)


def rank_blocks(shares_ref, out_ref):
    ranks = jnp.sum(shares_ref[...], axis=0).astype(jnp.bfloat16)
    for t in range(out_ref.shape[0]):
        out_ref[t] = ranks


def down_first(slots_ref, rows_ref, weight_ref, out_ref):
    width = weight_ref.shape[2]
    rows, tags = rows_ref[:, :width], rows_ref[:, width : width + 1].astype(jnp.float32)
    total = None
    for j in range(weight_ref.shape[0]):
        product = lax.dot_general(rows, weight_ref[j], NT, preferred_element_type=jnp.float32)
        mine = picked(slots_ref, tags, product, j)
        total = mine if total is None else total + mine
    write_packed(total, out_ref)


def tags_of(rows_ref, at, width):
    return rows_ref[:, at : at + width].astype(jnp.float32)


def grown(slots_ref, tags, ranks, pages, at, width):
    total = None
    for k, page in enumerate(pages):
        count, rank, _ = page.shape
        mine = [picked(slots_ref, tags, ranks, k * count + j) for j in range(count)]
        product = jnp.dot(
            jnp.concatenate(mine, axis=1).astype(jnp.bfloat16),
            page[:, :, at : at + width].reshape(count * rank, width),
            preferred_element_type=jnp.float32,
        )
        total = product if total is None else total + product
    return (adapter_scale * total).astype(jnp.bfloat16)


def up_first(slots_ref, ranks_ref, rows_ref, q_up, k_up, v_up, out_ref):
    rank = q_up.shape[1]
    tags = tags_of(rows_ref, rows_ref.shape[1] - 128, rank)
    ranks = read_packed(ranks_ref)
    at = 0
    for i, page in enumerate((q_up, k_up, v_up)):
        width = page.shape[2]
        mine = ranks[:, i * rank : (i + 1) * rank]
        out_ref[:, at : at + width] = grown(slots_ref, tags, mine, [page], 0, width)
        at += width


def term_blocks(from_y_ref, out_ref):
    out_ref[...] = summed(from_y_ref[...]).reshape(out_ref.shape).astype(jnp.bfloat16)


def make_down_second(at):
    def down_second(slots_ref, out_rows_ref, rows_ref, *refs):
        pages, out_ref = refs[:-1], refs[-1]
        count, rank, _ = pages[0].shape
        rows = out_rows_ref[...]
        tags = tags_of(rows_ref, rows_ref.shape[1] - 128, rank)
        total = jnp.zeros((rows.shape[0], rank), jnp.float32)
        for k, page in enumerate(pages):
            for j in range(count):
                weight = page[j, :, at : at + rows.shape[1]]
                product = lax.dot_general(rows, weight, NT, preferred_element_type=jnp.float32)
                total = total + picked(slots_ref, tags, product, k * count + j)
        half = rows.shape[0] // 2
        side = jnp.concatenate([total[:half], total[half:]], axis=1)
        for t in range(out_ref.shape[0]):
            out_ref[t] = side

    return down_second


def make_up_second(at):
    def up_second(slots_ref, parts_ref, rows_ref, *refs):
        pages, out_ref = refs[:-1], refs[-1]
        rank = pages[0].shape[1]
        side = jnp.sum(parts_ref[...], axis=0).astype(jnp.bfloat16).astype(jnp.float32)
        ranks = jnp.concatenate([side[:, :rank], side[:, rank:]], axis=0)
        tags = tags_of(rows_ref, rows_ref.shape[1] - 128, rank)
        out_ref[...] = grown(slots_ref, tags, ranks, pages, at, out_ref.shape[1])

    return up_second


def to_requests(rows):
    return summed(exchange(rows.reshape(lax.axis_size(Z), -1, rows.shape[1]), Z))


def body(
    hidden,
    q_base,
    base_key,
    base_value,
    paged_key_cache,
    paged_value_cache,
    page_table,
    context_len,
    adapter_id,
    adapter_slot,
    query_key_value_down,
    query_up_weight,
    key_up_weight,
    value_up_weight,
    output_down_weight,
    output_up_weight,
):
    local_rows, local_width = hidden.shape
    local_count = query_key_value_down.shape[0]
    y_size, z_size, t_size = lax.axis_size(Y), lax.axis_size(Z), lax.axis_size(T)
    rank, width_q, width_k = query_up_weight.shape[1], q_base.shape[1], base_key.shape[1]
    cuts = (0, width_q, width_q + width_k, width_q + 2 * width_k)
    own_y = lax.axis_index(Y)
    places = jnp.arange(y_size, dtype=jnp.int32)
    numbers = jnp.arange(local_count, dtype=jnp.int32)
    column_slots = (
        ((own_y - places[:, None]) % y_size * z_size + lax.axis_index(Z)) * local_count + numbers
    ).reshape(-1)

    def packed(*weights, after=()):
        width = sum(weight.shape[2] for weight in weights)
        shape = (local_count, rank, width)
        mine = call(pack, shape, jnp.bfloat16, *weights, scalars=0, after=after)
        return [mine] + [
            lax.ppermute(mine, Y, [(i, (i + k) % y_size) for i in range(y_size)])
            for k in range(1, y_size)
        ]

    z_blocks = pl.pallas_call(
        first_blocks,
        out_shape=jax.ShapeDtypeStruct((z_size, local_rows, local_width + 128), jnp.bfloat16),
        in_specs=[ANY] * 3,
        out_specs=VMEM,
        scratch_shapes=[
            pltpu.SMEM(adapter_id.shape, jnp.int32),
            pltpu.SMEM(adapter_slot.shape, jnp.int32),
            pltpu.VMEM(hidden.shape, jnp.bfloat16),
            pltpu.SemaphoreType.DMA((3,)),
        ],
    )(adapter_id, adapter_slot, hidden)
    y_blocks = call(
        second_blocks,
        (y_size, z_size * local_rows, local_width + 128),
        jnp.bfloat16,
        exchange(z_blocks, Z),
        scalars=0,
    )
    z_rows = y_blocks[0]
    all_rows = exchange(y_blocks, Y).reshape(y_size * z_size * local_rows, -1)

    packed_shape = (t_size, all_rows.shape[0] // t_size * 3 // 2, 2 * rank)
    part = call(
        down_first,
        packed_shape,
        jnp.float32,
        column_slots,
        all_rows,
        jnp.swapaxes(query_key_value_down, 1, 2),
    )
    ranks = exchange(
        call(rank_blocks, packed_shape, jnp.bfloat16, exchange(part, T), scalars=0), T
    )
    delta = call(
        up_first,
        (all_rows.shape[0], cuts[3]),
        jnp.bfloat16,
        column_slots,
        ranks,
        all_rows,
        query_up_weight,
        key_up_weight,
        value_up_weight,
    )
    from_y = exchange(delta.reshape(y_size, z_size * local_rows, cuts[3]), Y)
    terms = exchange(
        call(term_blocks, (z_size, local_rows, cuts[3]), jnp.bfloat16, from_y, scalars=0), Z
    )
    out_pages = packed(
        jnp.swapaxes(output_down_weight, 1, 2), output_up_weight, after=(from_y,)
    )
    attention, out_blocks = pl.pallas_call(
        attend,
        out_shape=[
            jax.ShapeDtypeStruct(q_base.shape, jnp.bfloat16),
            jax.ShapeDtypeStruct((z_size,) + q_base.shape, jnp.bfloat16),
        ],
        in_specs=[ANY] * 8,
        out_specs=[VMEM] * 2,
        scratch_shapes=[
            pltpu.SMEM(page_table.shape, jnp.int32),
            pltpu.SMEM(context_len.shape, jnp.int32),
            pltpu.VMEM(terms.shape, jnp.bfloat16),
            pltpu.VMEM(q_base.shape, jnp.bfloat16),
            pltpu.VMEM(base_key.shape, jnp.bfloat16),
            pltpu.VMEM(base_value.shape, jnp.bfloat16),
            pltpu.VMEM(paged_key_cache.shape, jnp.bfloat16),
            pltpu.VMEM(paged_value_cache.shape, jnp.bfloat16),
            pltpu.SemaphoreType.DMA((8,)),
        ],
        compiler_params=pltpu.CompilerParams(vmem_limit_bytes=32 * 2**20),
    )(
        page_table,
        context_len,
        terms,
        q_base,
        base_key,
        base_value,
        paged_key_cache,
        paged_value_cache,
    )
    out_rows = exchange(out_blocks, Z).reshape(z_size * local_rows, -1)
    sides = call(
        make_down_second(0),
        (t_size, z_size * local_rows // 2, 2 * rank),
        jnp.float32,
        column_slots,
        out_rows,
        z_rows,
        *out_pages,
    )
    term = call(
        make_up_second(local_width),
        (z_size * local_rows, output_up_weight.shape[2]),
        jnp.bfloat16,
        column_slots,
        exchange(sides, T),
        z_rows,
        *out_pages,
    )
    output_adapter_term = to_requests(term)
    return (attention, output_adapter_term.astype(jnp.bfloat16))


def solution(mesh):
    chips_y = 4
    wide, tensor = mesh.devices.shape
    devices = np.asarray(mesh.devices).reshape(chips_y, wide // chips_y, tensor)
    W = (Y, Z)
    return jax.shard_map(
        body,
        mesh=Mesh(devices, (Y, Z, T)),
        in_specs=(
            P(W, T),
            P(W, T),
            P(W, T),
            P(W, T),
            P(W, None, T),
            P(W, None, T),
            P(W, None),
            P(W),
            P(W),
            P(),
            P(W, T, None),
            P(W, None, T),
            P(W, None, T),
            P(W, None, T),
            P(W, T, None),
            P(W, None, T),
        ),
        out_specs=(P(W, T), P(W, T)),
        check_vma=False,
    )
```

```python
import jax
import jax.numpy as jnp
import numpy as np
from jax import lax
from jax.experimental import pallas as pl
from jax.experimental.pallas import tpu as pltpu
from jax.sharding import Mesh, PartitionSpec as P

adapter_scale = 2.0
Y, Z, T = "y", "z", "tensor"


def exchange(blocks, axis):
    return lax.all_to_all(blocks, axis, 0, 0)


def spread(block, axis):
    copies = jnp.broadcast_to(block[None], (lax.axis_size(axis),) + block.shape)
    return exchange(copies, axis)


def summed(parts):
    return jnp.sum(parts.astype(jnp.float32), axis=0)


NT = (((1,), (1,)), ((), ()))
VMEM = pl.BlockSpec(memory_space=pltpu.VMEM)
SMEM = pl.BlockSpec(memory_space=pltpu.SMEM)


ANY = pl.BlockSpec(memory_space=pl.ANY)


def call(kernel, shape, dtype, *operands, scalars=1, after=()):
    count = len(operands)

    def run(*refs):
        kernel(*refs[:count], *refs[count + len(after) :])

    return pl.pallas_call(
        run,
        out_shape=jax.ShapeDtypeStruct(shape, dtype),
        in_specs=[SMEM] * scalars + [VMEM] * (count - scalars) + [ANY] * len(after),
        out_specs=VMEM,
        compiler_params=pltpu.CompilerParams(vmem_limit_bytes=32 * 2**20),
    )(*operands, *after)


def fetch(sources, targets, sems):
    copies = [
        pltpu.make_async_copy(source, target, sems.at[i])
        for i, (source, target) in enumerate(zip(sources, targets))
    ]
    for copy in copies:
        copy.start()
    return copies


def first_blocks(id_hbm, slot_hbm, hidden_hbm, out_ref, id_ref, slot_ref, hidden_ref, sems):
    for copy in fetch((id_hbm, slot_hbm, hidden_hbm), (id_ref, slot_ref, hidden_ref), sems):
        copy.wait()
    rows, width = hidden_ref.shape
    tags = [
        jnp.full((1, 128), slot_ref[id_ref[r]].astype(jnp.float32), jnp.float32) for r in range(rows)
    ]
    block = jnp.concatenate(
        [hidden_ref[...], jnp.concatenate(tags, axis=0).astype(jnp.bfloat16)], axis=1
    )
    for z in range(out_ref.shape[0]):
        out_ref[z] = block


def attend(*refs):
    sources, (out_ref, block_ref), held, sems = refs[:8], refs[8:10], refs[10:18], refs[18]
    table_ref, length_ref, terms_ref, q_ref, k_ref, v_ref, keys_ref, values_ref = held
    copies = fetch(sources, held, sems)
    for copy in copies[:7]:
        copy.wait()
    rows, width_q = q_ref.shape
    size = k_ref.shape[1]
    heads = width_q // size
    delta = summed(terms_ref[...])
    parts = (
        q_ref[...].astype(jnp.float32) + delta[:, :width_q],
        k_ref[...].astype(jnp.float32) + delta[:, width_q : width_q + size],
        v_ref[...].astype(jnp.float32) + delta[:, width_q + size :],
    )
    query, key, value = [part.astype(jnp.bfloat16).astype(jnp.float32) for part in parts]
    inverse = 1.0 / size**0.5
    done = []
    for r in range(rows):
        pages = [table_ref[r, i] for i in range(table_ref.shape[1])]
        q = jnp.concatenate(
            [query[r : r + 1, h * size : (h + 1) * size] for h in range(heads)], axis=0
        )
        keys = jnp.concatenate([keys_ref[page] for page in pages], axis=0)
        scores = lax.dot_general(
            q.astype(jnp.bfloat16), keys, NT, preferred_element_type=jnp.float32
        )
        live = lax.broadcasted_iota(jnp.int32, scores.shape, 1) < length_ref[r]
        scores = jnp.where(live, scores * inverse, jnp.float32(-1e30))
        own = jnp.sum(q * key[r : r + 1], axis=1, keepdims=True) * inverse
        top = jnp.maximum(jnp.max(scores, axis=1, keepdims=True), own)
        weights = jnp.where(live, jnp.exp(scores - top), 0.0)
        own_weight = jnp.exp(own - top)
        total = jnp.sum(weights, axis=1, keepdims=True) + own_weight
        if r == 0:
            copies[7].wait()
        values = jnp.concatenate([values_ref[page] for page in pages], axis=0)
        mixed = jnp.dot(weights.astype(jnp.bfloat16), values, preferred_element_type=jnp.float32)
        own_rounded = own_weight.astype(jnp.bfloat16).astype(jnp.float32)
        mixed = (mixed + own_rounded * value[r : r + 1]) / total
        done.append(jnp.concatenate([mixed[h : h + 1] for h in range(heads)], axis=1))
    attention = jnp.concatenate(done, axis=0).astype(jnp.bfloat16)
    out_ref[...] = attention
    for z in range(block_ref.shape[0]):
        block_ref[z] = attention


def second_blocks(from_z_ref, out_ref):
    rows = from_z_ref[...].reshape(out_ref.shape[1:])
    for y in range(out_ref.shape[0]):
        out_ref[y] = rows


def pack(*refs):
    out_ref, at = refs[-1], 0
    for ref in refs[:-1]:
        out_ref[:, :, at : at + ref.shape[2]] = ref[...]
        at += ref.shape[2]


def picked(slots_ref, tags, values, number):
    return jnp.where(tags == slots_ref[number].astype(jnp.float32), values, jnp.zeros_like(values))


def write_packed(ranks, out_ref):
    shares, packed_rows, lanes = out_ref.shape
    rows = ranks.shape[0] // shares
    half = packed_rows - rows
    for t in range(shares):
        share = ranks[t * rows : (t + 1) * rows]
        out_ref[t, :rows] = share[:, :lanes]
        out_ref[t, rows:] = jnp.concatenate(
            [share[:half, lanes:], share[half:, lanes:]], axis=1
        )


def read_packed(packed):
    packed_rows, lanes = packed[0].shape
    rows = packed_rows * 2 // 3
    first, last = [], []
    for share in packed:
        first.append(share[:rows])
        last += [share[rows:, : lanes // 2], share[rows:, lanes // 2 :]]
    return jnp.concatenate([jnp.concatenate(first, 0), jnp.concatenate(last, 0)], axis=1)


def rank_blocks(shares_ref, out_ref):
    ranks = jnp.sum(shares_ref[...], axis=0).astype(jnp.bfloat16)
    for t in range(out_ref.shape[0]):
        out_ref[t] = ranks


def down_first(slots_ref, rows_ref, weight_ref, out_ref):
    width = weight_ref.shape[2]
    rows, tags = rows_ref[:, :width], rows_ref[:, width : width + 1].astype(jnp.float32)
    total = None
    for j in range(weight_ref.shape[0]):
        product = lax.dot_general(rows, weight_ref[j], NT, preferred_element_type=jnp.float32)
        mine = picked(slots_ref, tags, product, j)
        total = mine if total is None else total + mine
    write_packed(total, out_ref)


def tags_of(rows_ref, at, width):
    return rows_ref[:, at : at + width].astype(jnp.float32)


def grown(slots_ref, tags, ranks, pages, at, width):
    total = None
    for k, page in enumerate(pages):
        count, rank, _ = page.shape
        mine = [picked(slots_ref, tags, ranks, k * count + j) for j in range(count)]
        product = jnp.dot(
            jnp.concatenate(mine, axis=1).astype(jnp.bfloat16),
            page[:, :, at : at + width].reshape(count * rank, width),
            preferred_element_type=jnp.float32,
        )
        total = product if total is None else total + product
    return (adapter_scale * total).astype(jnp.bfloat16)


def make_up_first(cuts):
    def up_first(slots_ref, place_ref, ranks_ref, rows_ref, *refs):
        pages, out_ref = refs[:-1], refs[-1]
        y_size, shares = len(pages), ranks_ref.shape[0] // len(pages)
        mine = []
        for i in range(shares // y_size):
            share = place_ref[0] * (shares // y_size) + i
            parts = [ranks_ref[y * shares + share].astype(jnp.float32) for y in range(y_size)]
            mine.append(sum(parts[1:], parts[0]))
        ranks = read_packed(mine)
        rank = pages[0].shape[1]
        tags = tags_of(rows_ref, rows_ref.shape[1] - 128, rank)
        for i in range(3):
            width = cuts[i + 1] - cuts[i]
            values = ranks[:, i * rank : (i + 1) * rank]
            term = grown(slots_ref, tags, values, pages, cuts[i], width)
            blocks = term.astype(jnp.float32).reshape(out_ref.shape[:2] + (width,))
            out_ref[:, :, cuts[i] : cuts[i + 1]] = blocks.astype(jnp.bfloat16)

    return up_first


def make_down_second(at):
    def down_second(slots_ref, out_rows_ref, rows_ref, *refs):
        pages, out_ref = refs[:-1], refs[-1]
        count, rank, _ = pages[0].shape
        rows = out_rows_ref[...]
        tags = tags_of(rows_ref, rows_ref.shape[1] - 128, rank)
        total = jnp.zeros((rows.shape[0], rank), jnp.float32)
        for k, page in enumerate(pages):
            for j in range(count):
                weight = page[j, :, at : at + rows.shape[1]]
                product = lax.dot_general(rows, weight, NT, preferred_element_type=jnp.float32)
                total = total + picked(slots_ref, tags, product, k * count + j)
        half = rows.shape[0] // 2
        side = jnp.concatenate([total[:half], total[half:]], axis=1)
        for t in range(out_ref.shape[0]):
            out_ref[t] = side

    return down_second


def make_up_second(at):
    def up_second(slots_ref, parts_ref, rows_ref, *refs):
        pages, out_ref = refs[:-1], refs[-1]
        rank = pages[0].shape[1]
        side = jnp.sum(parts_ref[...], axis=0).astype(jnp.bfloat16).astype(jnp.float32)
        ranks = jnp.concatenate([side[:, :rank], side[:, rank:]], axis=0)
        tags = tags_of(rows_ref, rows_ref.shape[1] - 128, rank)
        out_ref[...] = grown(slots_ref, tags, ranks, pages, at, out_ref.shape[1])

    return up_second


def to_requests(rows):
    return summed(exchange(rows.reshape(lax.axis_size(Z), -1, rows.shape[1]), Z))


def body(
    hidden,
    q_base,
    base_key,
    base_value,
    paged_key_cache,
    paged_value_cache,
    page_table,
    context_len,
    adapter_id,
    adapter_slot,
    query_key_value_down,
    query_up_weight,
    key_up_weight,
    value_up_weight,
    output_down_weight,
    output_up_weight,
):
    local_rows, local_width = hidden.shape
    local_count = query_key_value_down.shape[0]
    y_size, z_size, t_size = lax.axis_size(Y), lax.axis_size(Z), lax.axis_size(T)
    rank, width_q, width_k = query_up_weight.shape[1], q_base.shape[1], base_key.shape[1]
    cuts = (0, width_q, width_q + width_k, width_q + 2 * width_k)
    own_y = lax.axis_index(Y)
    places = jnp.arange(y_size, dtype=jnp.int32)
    numbers = jnp.arange(local_count, dtype=jnp.int32)
    column_slots = (
        ((own_y - places[:, None]) % y_size * z_size + lax.axis_index(Z)) * local_count + numbers
    ).reshape(-1)

    def packed(*weights, after=()):
        width = sum(weight.shape[2] for weight in weights)
        shape = (local_count, rank, width)
        mine = call(pack, shape, jnp.bfloat16, *weights, scalars=0, after=after)
        return [mine] + [
            lax.ppermute(mine, Y, [(i, (i + k) % y_size) for i in range(y_size)])
            for k in range(1, y_size)
        ]

    up_pages = packed(query_up_weight, key_up_weight, value_up_weight)
    z_blocks = pl.pallas_call(
        first_blocks,
        out_shape=jax.ShapeDtypeStruct((z_size, local_rows, local_width + 128), jnp.bfloat16),
        in_specs=[ANY] * 3,
        out_specs=VMEM,
        scratch_shapes=[
            pltpu.SMEM(adapter_id.shape, jnp.int32),
            pltpu.SMEM(adapter_slot.shape, jnp.int32),
            pltpu.VMEM(hidden.shape, jnp.bfloat16),
            pltpu.SemaphoreType.DMA((3,)),
        ],
    )(adapter_id, adapter_slot, hidden)
    y_blocks = call(
        second_blocks,
        (y_size, z_size * local_rows, local_width + 128),
        jnp.bfloat16,
        exchange(z_blocks, Z),
        scalars=0,
        after=up_pages[1:2],
    )
    z_rows = y_blocks[0]
    all_rows = exchange(y_blocks, Y).reshape(y_size * z_size * local_rows, -1)

    packed_shape = (t_size, all_rows.shape[0] // t_size * 3 // 2, 2 * rank)
    part = call(
        down_first,
        packed_shape,
        jnp.float32,
        column_slots,
        all_rows,
        jnp.swapaxes(query_key_value_down, 1, 2),
    )
    ranks = exchange(
        call(
            rank_blocks,
            (y_size * t_size,) + packed_shape[1:],
            jnp.bfloat16,
            exchange(part, T),
            scalars=0,
            after=up_pages[2:],
        ),
        (Y, T),
    )
    blocks = call(
        make_up_first(cuts),
        (z_size, local_rows, cuts[3]),
        jnp.bfloat16,
        column_slots,
        own_y[None].astype(jnp.int32),
        ranks,
        z_rows,
        *up_pages,
        scalars=2,
    )
    terms = exchange(blocks, Z)
    out_pages = packed(
        jnp.swapaxes(output_down_weight, 1, 2), output_up_weight, after=(ranks,)
    )
    attention, out_blocks = pl.pallas_call(
        attend,
        out_shape=[
            jax.ShapeDtypeStruct(q_base.shape, jnp.bfloat16),
            jax.ShapeDtypeStruct((z_size,) + q_base.shape, jnp.bfloat16),
        ],
        in_specs=[ANY] * 8,
        out_specs=[VMEM] * 2,
        scratch_shapes=[
            pltpu.SMEM(page_table.shape, jnp.int32),
            pltpu.SMEM(context_len.shape, jnp.int32),
            pltpu.VMEM(terms.shape, jnp.bfloat16),
            pltpu.VMEM(q_base.shape, jnp.bfloat16),
            pltpu.VMEM(base_key.shape, jnp.bfloat16),
            pltpu.VMEM(base_value.shape, jnp.bfloat16),
            pltpu.VMEM(paged_key_cache.shape, jnp.bfloat16),
            pltpu.VMEM(paged_value_cache.shape, jnp.bfloat16),
            pltpu.SemaphoreType.DMA((8,)),
        ],
        compiler_params=pltpu.CompilerParams(vmem_limit_bytes=32 * 2**20),
    )(
        page_table,
        context_len,
        terms,
        q_base,
        base_key,
        base_value,
        paged_key_cache,
        paged_value_cache,
    )
    out_rows = exchange(out_blocks, Z).reshape(z_size * local_rows, -1)
    sides = call(
        make_down_second(0),
        (t_size, z_size * local_rows // 2, 2 * rank),
        jnp.float32,
        column_slots,
        out_rows,
        z_rows,
        *out_pages,
    )
    term = call(
        make_up_second(local_width),
        (z_size * local_rows, output_up_weight.shape[2]),
        jnp.bfloat16,
        column_slots,
        exchange(sides, T),
        z_rows,
        *out_pages,
    )
    output_adapter_term = to_requests(term)
    return (attention, output_adapter_term.astype(jnp.bfloat16))


def solution(mesh):
    chips_y = 4
    wide, tensor = mesh.devices.shape
    devices = np.asarray(mesh.devices).reshape(chips_y, wide // chips_y, tensor)
    W = (Y, Z)
    return jax.shard_map(
        body,
        mesh=Mesh(devices, (Y, Z, T)),
        in_specs=(
            P(W, T),
            P(W, T),
            P(W, T),
            P(W, T),
            P(W, None, T),
            P(W, None, T),
            P(W, None),
            P(W),
            P(W),
            P(),
            P(W, T, None),
            P(W, None, T),
            P(W, None, T),
            P(W, None, T),
            P(W, T, None),
            P(W, None, T),
        ),
        out_specs=(P(W, T), P(W, T)),
        check_vma=False,
    )
```

```python
import jax
import jax.numpy as jnp
import numpy as np
from jax import lax
from jax.experimental import pallas as pl
from jax.experimental.pallas import tpu as pltpu
from jax.sharding import Mesh, PartitionSpec as P

adapter_scale = 2.0
Y, Z, T = "y", "z", "tensor"


def exchange(blocks, axis):
    return lax.all_to_all(blocks, axis, 0, 0)


def spread(block, axis):
    copies = jnp.broadcast_to(block[None], (lax.axis_size(axis),) + block.shape)
    return exchange(copies, axis)


def summed(parts):
    return jnp.sum(parts.astype(jnp.float32), axis=0)


NT = (((1,), (1,)), ((), ()))
VMEM = pl.BlockSpec(memory_space=pltpu.VMEM)
SMEM = pl.BlockSpec(memory_space=pltpu.SMEM)


ANY = pl.BlockSpec(memory_space=pl.ANY)


def call(kernel, shape, dtype, *operands, scalars=1, after=()):
    count = len(operands)

    def run(*refs):
        kernel(*refs[:count], *refs[count + len(after) :])

    return pl.pallas_call(
        run,
        out_shape=jax.ShapeDtypeStruct(shape, dtype),
        in_specs=[SMEM] * scalars + [VMEM] * (count - scalars) + [ANY] * len(after),
        out_specs=VMEM,
        compiler_params=pltpu.CompilerParams(vmem_limit_bytes=32 * 2**20),
    )(*operands, *after)


def fetch(sources, targets, sems):
    copies = [
        pltpu.make_async_copy(source, target, sems.at[i])
        for i, (source, target) in enumerate(zip(sources, targets))
    ]
    for copy in copies:
        copy.start()
    return copies


def first_blocks(id_hbm, slot_hbm, hidden_hbm, out_ref, id_ref, slot_ref, hidden_ref, sems):
    for copy in fetch((id_hbm, slot_hbm, hidden_hbm), (id_ref, slot_ref, hidden_ref), sems):
        copy.wait()
    rows, width = hidden_ref.shape
    tags = [
        jnp.full((1, 128), slot_ref[id_ref[r]].astype(jnp.float32), jnp.float32) for r in range(rows)
    ]
    block = jnp.concatenate(
        [hidden_ref[...], jnp.concatenate(tags, axis=0).astype(jnp.bfloat16)], axis=1
    )
    for z in range(out_ref.shape[0]):
        out_ref[z] = block


def attend(*refs):
    sources, (out_ref, block_ref), held, sems = refs[:8], refs[8:10], refs[10:18], refs[18]
    table_ref, length_ref, terms_ref, q_ref, k_ref, v_ref, keys_ref, values_ref = held
    copies = fetch(sources, held, sems)
    for copy in copies[:7]:
        copy.wait()
    rows, width_q = q_ref.shape
    size = k_ref.shape[1]
    heads = width_q // size
    delta = summed(terms_ref[...])
    parts = (
        q_ref[...].astype(jnp.float32) + delta[:, :width_q],
        k_ref[...].astype(jnp.float32) + delta[:, width_q : width_q + size],
        v_ref[...].astype(jnp.float32) + delta[:, width_q + size :],
    )
    query, key, value = [part.astype(jnp.bfloat16).astype(jnp.float32) for part in parts]
    inverse = 1.0 / size**0.5
    done = []
    for r in range(rows):
        pages = [table_ref[r, i] for i in range(table_ref.shape[1])]
        q = jnp.concatenate(
            [query[r : r + 1, h * size : (h + 1) * size] for h in range(heads)], axis=0
        )
        keys = jnp.concatenate([keys_ref[page] for page in pages], axis=0)
        scores = lax.dot_general(
            q.astype(jnp.bfloat16), keys, NT, preferred_element_type=jnp.float32
        )
        live = lax.broadcasted_iota(jnp.int32, scores.shape, 1) < length_ref[r]
        scores = jnp.where(live, scores * inverse, jnp.float32(-1e30))
        own = jnp.sum(q * key[r : r + 1], axis=1, keepdims=True) * inverse
        top = jnp.maximum(jnp.max(scores, axis=1, keepdims=True), own)
        weights = jnp.where(live, jnp.exp(scores - top), 0.0)
        own_weight = jnp.exp(own - top)
        total = jnp.sum(weights, axis=1, keepdims=True) + own_weight
        if r == 0:
            copies[7].wait()
        values = jnp.concatenate([values_ref[page] for page in pages], axis=0)
        mixed = jnp.dot(weights.astype(jnp.bfloat16), values, preferred_element_type=jnp.float32)
        own_rounded = own_weight.astype(jnp.bfloat16).astype(jnp.float32)
        mixed = (mixed + own_rounded * value[r : r + 1]) / total
        done.append(jnp.concatenate([mixed[h : h + 1] for h in range(heads)], axis=1))
    attention = jnp.concatenate(done, axis=0).astype(jnp.bfloat16)
    out_ref[...] = attention
    for z in range(block_ref.shape[0]):
        block_ref[z] = attention


def second_blocks(from_z_ref, out_ref):
    rows = from_z_ref[...].reshape(out_ref.shape[1:])
    for y in range(out_ref.shape[0]):
        out_ref[y] = rows


def pack(*refs):
    out_ref, at = refs[-1], 0
    for ref in refs[:-1]:
        out_ref[:, :, at : at + ref.shape[2]] = ref[...]
        at += ref.shape[2]


def picked(slots_ref, tags, values, number):
    return jnp.where(tags == slots_ref[number].astype(jnp.float32), values, jnp.zeros_like(values))


def write_packed(ranks, out_ref):
    shares, packed_rows, lanes = out_ref.shape
    rows = ranks.shape[0] // shares
    half = packed_rows - rows
    for t in range(shares):
        share = ranks[t * rows : (t + 1) * rows]
        out_ref[t, :rows] = share[:, :lanes]
        out_ref[t, rows:] = jnp.concatenate(
            [share[:half, lanes:], share[half:, lanes:]], axis=1
        )


def read_packed(ref):
    shares, packed_rows, lanes = ref.shape
    rows = packed_rows * 2 // 3
    first, last = [], []
    for t in range(shares):
        share = ref[t].astype(jnp.float32)
        first.append(share[:rows])
        last += [share[rows:, : lanes // 2], share[rows:, lanes // 2 :]]
    return jnp.concatenate([jnp.concatenate(first, 0), jnp.concatenate(last, 0)], axis=1)


def rank_blocks(shares_ref, out_ref):
    ranks = jnp.sum(shares_ref[...], axis=0).astype(jnp.bfloat16)
    for t in range(out_ref.shape[0]):
        out_ref[t] = ranks


def down_first(slots_ref, rows_ref, weight_ref, out_ref):
    width = weight_ref.shape[2]
    rows, tags = rows_ref[:, :width], rows_ref[:, width : width + 1].astype(jnp.float32)
    total = None
    for j in range(weight_ref.shape[0]):
        product = lax.dot_general(rows, weight_ref[j], NT, preferred_element_type=jnp.float32)
        mine = picked(slots_ref, tags, product, j)
        total = mine if total is None else total + mine
    write_packed(total, out_ref)


def tags_of(rows_ref, at, width):
    return rows_ref[:, at : at + width].astype(jnp.float32)


def grown(slots_ref, tags, ranks, pages, at, width):
    total = None
    for k, page in enumerate(pages):
        count, rank, _ = page.shape
        mine = [picked(slots_ref, tags, ranks, k * count + j) for j in range(count)]
        product = jnp.dot(
            jnp.concatenate(mine, axis=1).astype(jnp.bfloat16),
            page[:, :, at : at + width].reshape(count * rank, width),
            preferred_element_type=jnp.float32,
        )
        total = product if total is None else total + product
    return (adapter_scale * total).astype(jnp.bfloat16)


def up_first(slots_ref, ranks_ref, rows_ref, q_up, k_up, v_up, out_ref):
    rank = q_up.shape[1]
    tags = tags_of(rows_ref, rows_ref.shape[1] - 128, rank)
    ranks = read_packed(ranks_ref)
    at = 0
    for i, page in enumerate((q_up, k_up, v_up)):
        width = page.shape[2]
        mine = ranks[:, i * rank : (i + 1) * rank]
        out_ref[:, at : at + width] = grown(slots_ref, tags, mine, [page], 0, width)
        at += width


def term_blocks(from_y_ref, out_ref):
    out_ref[...] = summed(from_y_ref[...]).reshape(out_ref.shape).astype(jnp.bfloat16)


def make_down_second(at):
    def down_second(slots_ref, out_rows_ref, rows_ref, *refs):
        pages, out_ref = refs[:-1], refs[-1]
        count, rank, _ = pages[0].shape
        rows = out_rows_ref[...]
        tags = tags_of(rows_ref, rows_ref.shape[1] - 128, rank)
        total = jnp.zeros((rows.shape[0], rank), jnp.float32)
        for k, page in enumerate(pages):
            for j in range(count):
                weight = page[j, :, at : at + rows.shape[1]]
                product = lax.dot_general(rows, weight, NT, preferred_element_type=jnp.float32)
                total = total + picked(slots_ref, tags, product, k * count + j)
        half = rows.shape[0] // 2
        side = jnp.concatenate([total[:half], total[half:]], axis=1)
        for t in range(out_ref.shape[0]):
            out_ref[t] = side

    return down_second


def make_up_second(at):
    def up_second(slots_ref, parts_ref, rows_ref, *refs):
        pages, out_ref = refs[:-1], refs[-1]
        rank = pages[0].shape[1]
        side = jnp.sum(parts_ref[...], axis=0).astype(jnp.bfloat16).astype(jnp.float32)
        ranks = jnp.concatenate([side[:, :rank], side[:, rank:]], axis=0)
        tags = tags_of(rows_ref, rows_ref.shape[1] - 128, rank)
        out_ref[...] = grown(slots_ref, tags, ranks, pages, at, out_ref.shape[1])

    return up_second


def to_requests(rows):
    return summed(exchange(rows.reshape(lax.axis_size(Z), -1, rows.shape[1]), Z))


def body(
    hidden,
    q_base,
    base_key,
    base_value,
    paged_key_cache,
    paged_value_cache,
    page_table,
    context_len,
    adapter_id,
    adapter_slot,
    query_key_value_down,
    query_up_weight,
    key_up_weight,
    value_up_weight,
    output_down_weight,
    output_up_weight,
):
    local_rows, local_width = hidden.shape
    local_count = query_key_value_down.shape[0]
    y_size, z_size, t_size = lax.axis_size(Y), lax.axis_size(Z), lax.axis_size(T)
    rank, width_q, width_k = query_up_weight.shape[1], q_base.shape[1], base_key.shape[1]
    cuts = (0, width_q, width_q + width_k, width_q + 2 * width_k)
    own_y = lax.axis_index(Y)
    places = jnp.arange(y_size, dtype=jnp.int32)
    numbers = jnp.arange(local_count, dtype=jnp.int32)
    column_slots = (
        ((own_y - places[:, None]) % y_size * z_size + lax.axis_index(Z)) * local_count + numbers
    ).reshape(-1)

    def packed_out(after):
        weights = (jnp.swapaxes(output_down_weight, 1, 2), output_up_weight)
        width = sum(weight.shape[2] for weight in weights)
        shape = (local_count, rank, width)
        return call(pack, shape, jnp.bfloat16, *weights, scalars=0, after=after)

    def shifted(page, k):
        return lax.ppermute(page, Y, [(i, (i + k) % y_size) for i in range(y_size)])

    z_blocks = pl.pallas_call(
        first_blocks,
        out_shape=jax.ShapeDtypeStruct((z_size, local_rows, local_width + 128), jnp.bfloat16),
        in_specs=[ANY] * 3,
        out_specs=VMEM,
        scratch_shapes=[
            pltpu.SMEM(adapter_id.shape, jnp.int32),
            pltpu.SMEM(adapter_slot.shape, jnp.int32),
            pltpu.VMEM(hidden.shape, jnp.bfloat16),
            pltpu.SemaphoreType.DMA((3,)),
        ],
    )(adapter_id, adapter_slot, hidden)
    y_blocks = call(
        second_blocks,
        (y_size, z_size * local_rows, local_width + 128),
        jnp.bfloat16,
        exchange(z_blocks, Z),
        scalars=0,
    )
    z_rows = y_blocks[0]
    all_rows = exchange(y_blocks, Y).reshape(y_size * z_size * local_rows, -1)

    early = packed_out((y_blocks,))
    near = [shifted(early, 1), shifted(early, y_size - 1)]
    packed_shape = (t_size, all_rows.shape[0] // t_size * 3 // 2, 2 * rank)
    part = call(
        down_first,
        packed_shape,
        jnp.float32,
        column_slots,
        all_rows,
        jnp.swapaxes(query_key_value_down, 1, 2),
    )
    ranks = exchange(
        call(rank_blocks, packed_shape, jnp.bfloat16, exchange(part, T), scalars=0, after=near), T
    )
    delta = call(
        up_first,
        (all_rows.shape[0], cuts[3]),
        jnp.bfloat16,
        column_slots,
        ranks,
        all_rows,
        query_up_weight,
        key_up_weight,
        value_up_weight,
    )
    from_y = exchange(delta.reshape(y_size, z_size * local_rows, cuts[3]), Y)
    terms = exchange(
        call(term_blocks, (z_size, local_rows, cuts[3]), jnp.bfloat16, from_y, scalars=0), Z
    )
    late = packed_out((from_y,))
    out_pages = [early, near[0], shifted(late, 2), near[1]]
    attention, out_blocks = pl.pallas_call(
        attend,
        out_shape=[
            jax.ShapeDtypeStruct(q_base.shape, jnp.bfloat16),
            jax.ShapeDtypeStruct((z_size,) + q_base.shape, jnp.bfloat16),
        ],
        in_specs=[ANY] * 8,
        out_specs=[VMEM] * 2,
        scratch_shapes=[
            pltpu.SMEM(page_table.shape, jnp.int32),
            pltpu.SMEM(context_len.shape, jnp.int32),
            pltpu.VMEM(terms.shape, jnp.bfloat16),
            pltpu.VMEM(q_base.shape, jnp.bfloat16),
            pltpu.VMEM(base_key.shape, jnp.bfloat16),
            pltpu.VMEM(base_value.shape, jnp.bfloat16),
            pltpu.VMEM(paged_key_cache.shape, jnp.bfloat16),
            pltpu.VMEM(paged_value_cache.shape, jnp.bfloat16),
            pltpu.SemaphoreType.DMA((8,)),
        ],
        compiler_params=pltpu.CompilerParams(vmem_limit_bytes=32 * 2**20),
    )(
        page_table,
        context_len,
        terms,
        q_base,
        base_key,
        base_value,
        paged_key_cache,
        paged_value_cache,
    )
    out_rows = exchange(out_blocks, Z).reshape(z_size * local_rows, -1)
    sides = call(
        make_down_second(0),
        (t_size, z_size * local_rows // 2, 2 * rank),
        jnp.float32,
        column_slots,
        out_rows,
        z_rows,
        *out_pages,
    )
    term = call(
        make_up_second(local_width),
        (z_size * local_rows, output_up_weight.shape[2]),
        jnp.bfloat16,
        column_slots,
        exchange(sides, T),
        z_rows,
        *out_pages,
    )
    output_adapter_term = to_requests(term)
    return (attention, output_adapter_term.astype(jnp.bfloat16))


def solution(mesh):
    chips_y = 4
    wide, tensor = mesh.devices.shape
    devices = np.asarray(mesh.devices).reshape(chips_y, wide // chips_y, tensor)
    W = (Y, Z)
    return jax.shard_map(
        body,
        mesh=Mesh(devices, (Y, Z, T)),
        in_specs=(
            P(W, T),
            P(W, T),
            P(W, T),
            P(W, T),
            P(W, None, T),
            P(W, None, T),
            P(W, None),
            P(W),
            P(W),
            P(),
            P(W, T, None),
            P(W, None, T),
            P(W, None, T),
            P(W, None, T),
            P(W, T, None),
            P(W, None, T),
        ),
        out_specs=(P(W, T), P(W, T)),
        check_vma=False,
    )
```

```python
import jax
import jax.numpy as jnp
import numpy as np
from jax import lax
from jax.experimental import pallas as pl
from jax.experimental.pallas import tpu as pltpu
from jax.sharding import Mesh, PartitionSpec as P

adapter_scale = 2.0
Y, Z, T = "y", "z", "tensor"


def exchange(blocks, axis):
    return lax.all_to_all(blocks, axis, 0, 0)


def spread(block, axis):
    copies = jnp.broadcast_to(block[None], (lax.axis_size(axis),) + block.shape)
    return exchange(copies, axis)


def summed(parts):
    return jnp.sum(parts.astype(jnp.float32), axis=0)


NT = (((1,), (1,)), ((), ()))
VMEM = pl.BlockSpec(memory_space=pltpu.VMEM)
SMEM = pl.BlockSpec(memory_space=pltpu.SMEM)


ANY = pl.BlockSpec(memory_space=pl.ANY)


def call(kernel, shape, dtype, *operands, scalars=1, after=()):
    count = len(operands)

    def run(*refs):
        kernel(*refs[:count], *refs[count + len(after) :])

    return pl.pallas_call(
        run,
        out_shape=jax.ShapeDtypeStruct(shape, dtype),
        in_specs=[SMEM] * scalars + [VMEM] * (count - scalars) + [ANY] * len(after),
        out_specs=VMEM,
        compiler_params=pltpu.CompilerParams(vmem_limit_bytes=32 * 2**20),
    )(*operands, *after)


def fetch(sources, targets, sems):
    copies = [
        pltpu.make_async_copy(source, target, sems.at[i])
        for i, (source, target) in enumerate(zip(sources, targets))
    ]
    for copy in copies:
        copy.start()
    return copies


def first_blocks(id_hbm, slot_hbm, hidden_hbm, out_ref, id_ref, slot_ref, hidden_ref, sems):
    for copy in fetch((id_hbm, slot_hbm, hidden_hbm), (id_ref, slot_ref, hidden_ref), sems):
        copy.wait()
    rows, width = hidden_ref.shape
    tags = [
        jnp.full((1, 128), slot_ref[id_ref[r]].astype(jnp.float32), jnp.float32) for r in range(rows)
    ]
    block = jnp.concatenate(
        [hidden_ref[...], jnp.concatenate(tags, axis=0).astype(jnp.bfloat16)], axis=1
    )
    for z in range(out_ref.shape[0]):
        out_ref[z] = block


def attend(*refs):
    sources, (out_ref, block_ref), held, sems = refs[:8], refs[8:10], refs[10:18], refs[18]
    table_ref, length_ref, terms_ref, q_ref, k_ref, v_ref, keys_ref, values_ref = held
    copies = fetch(sources, held, sems)
    for copy in copies[:7]:
        copy.wait()
    rows, width_q = q_ref.shape
    size = k_ref.shape[1]
    heads = width_q // size
    delta = summed(terms_ref[...])
    parts = (
        q_ref[...].astype(jnp.float32) + delta[:, :width_q],
        k_ref[...].astype(jnp.float32) + delta[:, width_q : width_q + size],
        v_ref[...].astype(jnp.float32) + delta[:, width_q + size :],
    )
    query, key, value = [part.astype(jnp.bfloat16).astype(jnp.float32) for part in parts]
    inverse = 1.0 / size**0.5
    done = []
    for r in range(rows):
        pages = [table_ref[r, i] for i in range(table_ref.shape[1])]
        q = jnp.concatenate(
            [query[r : r + 1, h * size : (h + 1) * size] for h in range(heads)], axis=0
        )
        keys = jnp.concatenate([keys_ref[page] for page in pages], axis=0)
        scores = lax.dot_general(
            q.astype(jnp.bfloat16), keys, NT, preferred_element_type=jnp.float32
        )
        live = lax.broadcasted_iota(jnp.int32, scores.shape, 1) < length_ref[r]
        scores = jnp.where(live, scores * inverse, jnp.float32(-1e30))
        own = jnp.sum(q * key[r : r + 1], axis=1, keepdims=True) * inverse
        top = jnp.maximum(jnp.max(scores, axis=1, keepdims=True), own)
        weights = jnp.where(live, jnp.exp(scores - top), 0.0)
        own_weight = jnp.exp(own - top)
        total = jnp.sum(weights, axis=1, keepdims=True) + own_weight
        if r == 0:
            copies[7].wait()
        values = jnp.concatenate([values_ref[page] for page in pages], axis=0)
        mixed = jnp.dot(weights.astype(jnp.bfloat16), values, preferred_element_type=jnp.float32)
        own_rounded = own_weight.astype(jnp.bfloat16).astype(jnp.float32)
        mixed = (mixed + own_rounded * value[r : r + 1]) / total
        done.append(jnp.concatenate([mixed[h : h + 1] for h in range(heads)], axis=1))
    attention = jnp.concatenate(done, axis=0).astype(jnp.bfloat16)
    out_ref[...] = attention
    for z in range(block_ref.shape[0]):
        block_ref[z] = attention


def second_blocks(from_z_ref, out_ref):
    rows = from_z_ref[...].reshape(out_ref.shape[1:])
    for y in range(out_ref.shape[0]):
        out_ref[y] = rows


def pack(*refs):
    out_ref, at = refs[-1], 0
    for ref in refs[:-1]:
        out_ref[:, :, at : at + ref.shape[2]] = ref[...]
        at += ref.shape[2]


def picked(slots_ref, tags, values, number):
    return jnp.where(tags == slots_ref[number].astype(jnp.float32), values, jnp.zeros_like(values))


def write_packed(ranks, out_ref):
    shares, packed_rows, lanes = out_ref.shape
    rows = ranks.shape[0] // shares
    half = packed_rows - rows
    for t in range(shares):
        share = ranks[t * rows : (t + 1) * rows]
        out_ref[t, :rows] = share[:, :lanes]
        out_ref[t, rows:] = jnp.concatenate(
            [share[:half, lanes:], share[half:, lanes:]], axis=1
        )


def read_packed(ref):
    shares, packed_rows, lanes = ref.shape
    rows = packed_rows * 2 // 3
    first, last = [], []
    for t in range(shares):
        share = ref[t].astype(jnp.float32)
        first.append(share[:rows])
        last += [share[rows:, : lanes // 2], share[rows:, lanes // 2 :]]
    return jnp.concatenate([jnp.concatenate(first, 0), jnp.concatenate(last, 0)], axis=1)


def rank_blocks(shares_ref, out_ref):
    ranks = jnp.sum(shares_ref[...], axis=0).astype(jnp.bfloat16)
    for t in range(out_ref.shape[0]):
        out_ref[t] = ranks


def down_first(slots_ref, rows_ref, weight_ref, out_ref):
    width = weight_ref.shape[2]
    rows, tags = rows_ref[:, :width], rows_ref[:, width : width + 1].astype(jnp.float32)
    total = None
    for j in range(weight_ref.shape[0]):
        product = lax.dot_general(rows, weight_ref[j], NT, preferred_element_type=jnp.float32)
        mine = picked(slots_ref, tags, product, j)
        total = mine if total is None else total + mine
    write_packed(total, out_ref)


def tags_of(rows_ref, at, width):
    return rows_ref[:, at : at + width].astype(jnp.float32)


def grown(slots_ref, tags, ranks, pages, at, width):
    total = None
    for k, page in enumerate(pages):
        count, rank, _ = page.shape
        mine = [picked(slots_ref, tags, ranks, k * count + j) for j in range(count)]
        product = jnp.dot(
            jnp.concatenate(mine, axis=1).astype(jnp.bfloat16),
            page[:, :, at : at + width].reshape(count * rank, width),
            preferred_element_type=jnp.float32,
        )
        total = product if total is None else total + product
    return (adapter_scale * total).astype(jnp.bfloat16)


def up_first(slots_ref, ranks_ref, rows_ref, q_up, k_up, v_up, out_ref):
    rank = q_up.shape[1]
    tags = tags_of(rows_ref, rows_ref.shape[1] - 128, rank)
    ranks = read_packed(ranks_ref)
    at = 0
    for i, page in enumerate((q_up, k_up, v_up)):
        width = page.shape[2]
        mine = ranks[:, i * rank : (i + 1) * rank]
        out_ref[:, at : at + width] = grown(slots_ref, tags, mine, [page], 0, width)
        at += width


def term_blocks(from_y_ref, out_ref):
    out_ref[...] = summed(from_y_ref[...]).reshape(out_ref.shape).astype(jnp.bfloat16)


def make_down_second(at):
    def down_second(slots_ref, out_rows_ref, rows_ref, *refs):
        pages, out_ref = refs[:-1], refs[-1]
        count, rank, _ = pages[0].shape
        rows = out_rows_ref[...]
        tags = tags_of(rows_ref, rows_ref.shape[1] - 128, rank)
        total = jnp.zeros((rows.shape[0], rank), jnp.float32)
        for k, page in enumerate(pages):
            for j in range(count):
                weight = page[j, :, at : at + rows.shape[1]]
                product = lax.dot_general(rows, weight, NT, preferred_element_type=jnp.float32)
                total = total + picked(slots_ref, tags, product, k * count + j)
        half = rows.shape[0] // 2
        side = jnp.concatenate([total[:half], total[half:]], axis=1)
        for t in range(out_ref.shape[0]):
            out_ref[t] = side

    return down_second


def make_up_second(at):
    def up_second(slots_ref, parts_ref, rows_ref, *refs):
        pages, out_ref = refs[:-1], refs[-1]
        rank = pages[0].shape[1]
        side = jnp.sum(parts_ref[...], axis=0).astype(jnp.bfloat16).astype(jnp.float32)
        ranks = jnp.concatenate([side[:, :rank], side[:, rank:]], axis=0)
        tags = tags_of(rows_ref, rows_ref.shape[1] - 128, rank)
        out_ref[...] = grown(slots_ref, tags, ranks, pages, at, out_ref.shape[1])

    return up_second


def to_requests(rows):
    return summed(exchange(rows.reshape(lax.axis_size(Z), -1, rows.shape[1]), Z))


def body(
    hidden,
    q_base,
    base_key,
    base_value,
    paged_key_cache,
    paged_value_cache,
    page_table,
    context_len,
    adapter_id,
    adapter_slot,
    query_key_value_down,
    query_up_weight,
    key_up_weight,
    value_up_weight,
    output_down_weight,
    output_up_weight,
):
    local_rows, local_width = hidden.shape
    local_count = query_key_value_down.shape[0]
    y_size, z_size, t_size = lax.axis_size(Y), lax.axis_size(Z), lax.axis_size(T)
    rank, width_q, width_k = query_up_weight.shape[1], q_base.shape[1], base_key.shape[1]
    cuts = (0, width_q, width_q + width_k, width_q + 2 * width_k)
    own_y = lax.axis_index(Y)
    places = jnp.arange(y_size, dtype=jnp.int32)
    numbers = jnp.arange(local_count, dtype=jnp.int32)
    column_slots = (
        ((own_y - places[:, None]) % y_size * z_size + lax.axis_index(Z)) * local_count + numbers
    ).reshape(-1)

    def packed(*weights, after=()):
        width = sum(weight.shape[2] for weight in weights)
        shape = (local_count, rank, width)
        mine = call(pack, shape, jnp.bfloat16, *weights, scalars=0, after=after)
        return [mine] + [
            lax.ppermute(mine, Y, [(i, (i + k) % y_size) for i in range(y_size)])
            for k in range(1, y_size)
        ]

    z_blocks = pl.pallas_call(
        first_blocks,
        out_shape=jax.ShapeDtypeStruct((z_size, local_rows, local_width + 128), jnp.bfloat16),
        in_specs=[ANY] * 3,
        out_specs=VMEM,
        scratch_shapes=[
            pltpu.SMEM(adapter_id.shape, jnp.int32),
            pltpu.SMEM(adapter_slot.shape, jnp.int32),
            pltpu.VMEM(hidden.shape, jnp.bfloat16),
            pltpu.SemaphoreType.DMA((3,)),
        ],
    )(adapter_id, adapter_slot, hidden)
    y_blocks = call(
        second_blocks,
        (y_size, z_size * local_rows, local_width + 128),
        jnp.bfloat16,
        exchange(z_blocks, Z),
        scalars=0,
    )
    z_rows = y_blocks[0]
    all_rows = exchange(y_blocks, Y).reshape(y_size * z_size * local_rows, -1)

    packed_shape = (t_size, all_rows.shape[0] // t_size * 3 // 2, 2 * rank)
    part = call(
        down_first,
        packed_shape,
        jnp.float32,
        column_slots,
        all_rows,
        jnp.swapaxes(query_key_value_down, 1, 2),
    )
    ranks = exchange(
        call(rank_blocks, packed_shape, jnp.bfloat16, exchange(part, T), scalars=0), T
    )
    delta = call(
        up_first,
        (all_rows.shape[0], cuts[3]),
        jnp.bfloat16,
        column_slots,
        ranks,
        all_rows,
        query_up_weight,
        key_up_weight,
        value_up_weight,
    )
    from_y = exchange(delta.reshape(y_size, z_size * local_rows, cuts[3]), Y)
    terms = exchange(
        call(term_blocks, (z_size, local_rows, cuts[3]), jnp.bfloat16, from_y, scalars=0), Z
    )
    out_pages = packed(
        jnp.swapaxes(output_down_weight, 1, 2), output_up_weight, after=(from_y,)
    )
    attention, out_blocks = pl.pallas_call(
        attend,
        out_shape=[
            jax.ShapeDtypeStruct(q_base.shape, jnp.bfloat16),
            jax.ShapeDtypeStruct((z_size,) + q_base.shape, jnp.bfloat16),
        ],
        in_specs=[ANY] * 8,
        out_specs=[VMEM] * 2,
        scratch_shapes=[
            pltpu.SMEM(page_table.shape, jnp.int32),
            pltpu.SMEM(context_len.shape, jnp.int32),
            pltpu.VMEM(terms.shape, jnp.bfloat16),
            pltpu.VMEM(q_base.shape, jnp.bfloat16),
            pltpu.VMEM(base_key.shape, jnp.bfloat16),
            pltpu.VMEM(base_value.shape, jnp.bfloat16),
            pltpu.VMEM(paged_key_cache.shape, jnp.bfloat16),
            pltpu.VMEM(paged_value_cache.shape, jnp.bfloat16),
            pltpu.SemaphoreType.DMA((8,)),
        ],
        compiler_params=pltpu.CompilerParams(vmem_limit_bytes=52 * 2**20),
    )(
        page_table,
        context_len,
        terms,
        q_base,
        base_key,
        base_value,
        paged_key_cache,
        paged_value_cache,
    )
    out_rows = exchange(out_blocks, Z).reshape(z_size * local_rows, -1)
    sides = call(
        make_down_second(0),
        (t_size, z_size * local_rows // 2, 2 * rank),
        jnp.float32,
        column_slots,
        out_rows,
        z_rows,
        *out_pages,
    )
    term = call(
        make_up_second(local_width),
        (z_size * local_rows, output_up_weight.shape[2]),
        jnp.bfloat16,
        column_slots,
        exchange(sides, T),
        z_rows,
        *out_pages,
    )
    output_adapter_term = to_requests(term)
    return (attention, output_adapter_term.astype(jnp.bfloat16))


def solution(mesh):
    chips_y = 4
    wide, tensor = mesh.devices.shape
    devices = np.asarray(mesh.devices).reshape(chips_y, wide // chips_y, tensor)
    W = (Y, Z)
    return jax.shard_map(
        body,
        mesh=Mesh(devices, (Y, Z, T)),
        in_specs=(
            P(W, T),
            P(W, T),
            P(W, T),
            P(W, T),
            P(W, None, T),
            P(W, None, T),
            P(W, None),
            P(W),
            P(W),
            P(),
            P(W, T, None),
            P(W, None, T),
            P(W, None, T),
            P(W, None, T),
            P(W, T, None),
            P(W, None, T),
        ),
        out_specs=(P(W, T), P(W, T)),
        check_vma=False,
    )
```

```python
import jax
import jax.numpy as jnp
import numpy as np
from jax import lax
from jax.experimental import pallas as pl
from jax.experimental.pallas import tpu as pltpu
from jax.sharding import Mesh, PartitionSpec as P

adapter_scale = 2.0
Y, Z, T = "y", "z", "tensor"


def exchange(blocks, axis):
    return lax.all_to_all(blocks, axis, 0, 0)


def spread(block, axis):
    copies = jnp.broadcast_to(block[None], (lax.axis_size(axis),) + block.shape)
    return exchange(copies, axis)


def summed(parts):
    return jnp.sum(parts.astype(jnp.float32), axis=0)


NT = (((1,), (1,)), ((), ()))
VMEM = pl.BlockSpec(memory_space=pltpu.VMEM)
SMEM = pl.BlockSpec(memory_space=pltpu.SMEM)


ANY = pl.BlockSpec(memory_space=pl.ANY)


def call(kernel, shape, dtype, *operands, scalars=1, after=()):
    count = len(operands)

    def run(*refs):
        kernel(*refs[:count], *refs[count + len(after) :])

    return pl.pallas_call(
        run,
        out_shape=jax.ShapeDtypeStruct(shape, dtype),
        in_specs=[SMEM] * scalars + [VMEM] * (count - scalars) + [ANY] * len(after),
        out_specs=VMEM,
        compiler_params=pltpu.CompilerParams(vmem_limit_bytes=32 * 2**20),
    )(*operands, *after)


def fetch(sources, targets, sems):
    copies = [
        pltpu.make_async_copy(source, target, sems.at[i])
        for i, (source, target) in enumerate(zip(sources, targets))
    ]
    for copy in copies:
        copy.start()
    return copies


def first_blocks(id_hbm, slot_hbm, hidden_hbm, out_ref, id_ref, slot_ref, hidden_ref, sems):
    for copy in fetch((id_hbm, slot_hbm, hidden_hbm), (id_ref, slot_ref, hidden_ref), sems):
        copy.wait()
    rows, width = hidden_ref.shape
    tags = [
        jnp.full((1, 128), slot_ref[id_ref[r]].astype(jnp.float32), jnp.float32) for r in range(rows)
    ]
    block = jnp.concatenate(
        [hidden_ref[...], jnp.concatenate(tags, axis=0).astype(jnp.bfloat16)], axis=1
    )
    for z in range(out_ref.shape[0]):
        out_ref[z] = block


def attend(*refs):
    sources, (out_ref, block_ref), held, sems = refs[:8], refs[8:10], refs[10:18], refs[18]
    table_ref, length_ref, terms_ref, q_ref, k_ref, v_ref, keys_ref, values_ref = held
    copies = fetch(sources, held, sems)
    for copy in copies[:7]:
        copy.wait()
    rows, width_q = q_ref.shape
    size = k_ref.shape[1]
    heads = width_q // size
    delta = summed(terms_ref[...])
    parts = (
        q_ref[...].astype(jnp.float32) + delta[:, :width_q],
        k_ref[...].astype(jnp.float32) + delta[:, width_q : width_q + size],
        v_ref[...].astype(jnp.float32) + delta[:, width_q + size :],
    )
    query, key, value = [part.astype(jnp.bfloat16).astype(jnp.float32) for part in parts]
    inverse = 1.0 / size**0.5
    done = []
    for r in range(rows):
        pages = [table_ref[r, i] for i in range(table_ref.shape[1])]
        q = jnp.concatenate(
            [query[r : r + 1, h * size : (h + 1) * size] for h in range(heads)], axis=0
        )
        keys = jnp.concatenate([keys_ref[page] for page in pages], axis=0)
        scores = lax.dot_general(
            q.astype(jnp.bfloat16), keys, NT, preferred_element_type=jnp.float32
        )
        live = lax.broadcasted_iota(jnp.int32, scores.shape, 1) < length_ref[r]
        scores = jnp.where(live, scores * inverse, jnp.float32(-1e30))
        own = jnp.sum(q * key[r : r + 1], axis=1, keepdims=True) * inverse
        top = jnp.maximum(jnp.max(scores, axis=1, keepdims=True), own)
        weights = jnp.where(live, jnp.exp(scores - top), 0.0)
        own_weight = jnp.exp(own - top)
        total = jnp.sum(weights, axis=1, keepdims=True) + own_weight
        if r == 0:
            copies[7].wait()
        values = jnp.concatenate([values_ref[page] for page in pages], axis=0)
        mixed = jnp.dot(weights.astype(jnp.bfloat16), values, preferred_element_type=jnp.float32)
        own_rounded = own_weight.astype(jnp.bfloat16).astype(jnp.float32)
        mixed = (mixed + own_rounded * value[r : r + 1]) / total
        done.append(jnp.concatenate([mixed[h : h + 1] for h in range(heads)], axis=1))
    attention = jnp.concatenate(done, axis=0).astype(jnp.bfloat16)
    out_ref[...] = attention
    for z in range(block_ref.shape[0]):
        block_ref[z] = attention


def second_blocks(from_z_ref, out_ref):
    rows = from_z_ref[...].reshape(out_ref.shape[1:])
    for y in range(out_ref.shape[0]):
        out_ref[y] = rows


def pack(*refs):
    out_ref, at = refs[-1], 0
    for ref in refs[:-1]:
        out_ref[:, :, at : at + ref.shape[2]] = ref[...]
        at += ref.shape[2]


def picked(slots_ref, tags, values, number):
    return jnp.where(tags == slots_ref[number].astype(jnp.float32), values, jnp.zeros_like(values))


def write_packed(ranks, out_ref):
    shares, packed_rows, lanes = out_ref.shape
    rows = ranks.shape[0] // shares
    half = packed_rows - rows
    for t in range(shares):
        share = ranks[t * rows : (t + 1) * rows]
        out_ref[t, :rows] = share[:, :lanes]
        out_ref[t, rows:] = jnp.concatenate(
            [share[:half, lanes:], share[half:, lanes:]], axis=1
        )


def read_packed(ref):
    shares, packed_rows, lanes = ref.shape
    rows = packed_rows * 2 // 3
    first, last = [], []
    for t in range(shares):
        share = ref[t].astype(jnp.float32)
        first.append(share[:rows])
        last += [share[rows:, : lanes // 2], share[rows:, lanes // 2 :]]
    return jnp.concatenate([jnp.concatenate(first, 0), jnp.concatenate(last, 0)], axis=1)


def rank_blocks(shares_ref, out_ref):
    ranks = jnp.sum(shares_ref[...], axis=0).astype(jnp.bfloat16)
    for t in range(out_ref.shape[0]):
        out_ref[t] = ranks


def down_first(slots_ref, rows_ref, weight_ref, out_ref):
    width = weight_ref.shape[2]
    rows, tags = rows_ref[:, :width], rows_ref[:, width : width + 1].astype(jnp.float32)
    total = None
    for j in range(weight_ref.shape[0]):
        product = lax.dot_general(rows, weight_ref[j], NT, preferred_element_type=jnp.float32)
        mine = picked(slots_ref, tags, product, j)
        total = mine if total is None else total + mine
    write_packed(total, out_ref)


def tags_of(rows_ref, at, width):
    return rows_ref[:, at : at + width].astype(jnp.float32)


def grown(slots_ref, tags, ranks, pages, at, width):
    total = None
    for k, page in enumerate(pages):
        count, rank, _ = page.shape
        mine = [picked(slots_ref, tags, ranks, k * count + j) for j in range(count)]
        product = jnp.dot(
            jnp.concatenate(mine, axis=1).astype(jnp.bfloat16),
            page[:, :, at : at + width].reshape(count * rank, width),
            preferred_element_type=jnp.float32,
        )
        total = product if total is None else total + product
    return (adapter_scale * total).astype(jnp.bfloat16)


def up_first(slots_ref, ranks_ref, rows_ref, q_up, k_up, v_up, out_ref):
    rank = q_up.shape[1]
    tags = tags_of(rows_ref, rows_ref.shape[1] - 128, rank)
    ranks = read_packed(ranks_ref)
    at = 0
    for i, page in enumerate((q_up, k_up, v_up)):
        width = page.shape[2]
        mine = ranks[:, i * rank : (i + 1) * rank]
        out_ref[:, at : at + width] = grown(slots_ref, tags, mine, [page], 0, width)
        at += width


def term_blocks(from_y_ref, out_ref):
    out_ref[...] = summed(from_y_ref[...]).reshape(out_ref.shape).astype(jnp.bfloat16)


def make_down_second(at):
    def down_second(slots_ref, out_rows_ref, rows_ref, *refs):
        pages, out_ref = refs[:-1], refs[-1]
        count, rank, _ = pages[0].shape
        rows = out_rows_ref[...]
        tags = tags_of(rows_ref, rows_ref.shape[1] - 128, rank)
        total = jnp.zeros((rows.shape[0], rank), jnp.float32)
        for k, page in enumerate(pages):
            for j in range(count):
                weight = page[j, :, at : at + rows.shape[1]]
                product = lax.dot_general(rows, weight, NT, preferred_element_type=jnp.float32)
                total = total + picked(slots_ref, tags, product, k * count + j)
        half = rows.shape[0] // 2
        side = jnp.concatenate([total[:half], total[half:]], axis=1)
        for t in range(out_ref.shape[0]):
            out_ref[t] = side

    return down_second


def make_up_second(at):
    def up_second(slots_ref, parts_ref, rows_ref, *refs):
        pages, out_ref = refs[:-1], refs[-1]
        rank = pages[0].shape[1]
        side = jnp.sum(parts_ref[...], axis=0).astype(jnp.bfloat16).astype(jnp.float32)
        ranks = jnp.concatenate([side[:, :rank], side[:, rank:]], axis=0)
        tags = tags_of(rows_ref, rows_ref.shape[1] - 128, rank)
        out_ref[...] = grown(slots_ref, tags, ranks, pages, at, out_ref.shape[1])

    return up_second


def to_requests(rows):
    return summed(exchange(rows.reshape(lax.axis_size(Z), -1, rows.shape[1]), Z))


def body(
    hidden,
    q_base,
    base_key,
    base_value,
    paged_key_cache,
    paged_value_cache,
    page_table,
    context_len,
    adapter_id,
    adapter_slot,
    query_key_value_down,
    query_up_weight,
    key_up_weight,
    value_up_weight,
    output_down_weight,
    output_up_weight,
):
    local_rows, local_width = hidden.shape
    local_count = query_key_value_down.shape[0]
    y_size, z_size, t_size = lax.axis_size(Y), lax.axis_size(Z), lax.axis_size(T)
    rank, width_q, width_k = query_up_weight.shape[1], q_base.shape[1], base_key.shape[1]
    cuts = (0, width_q, width_q + width_k, width_q + 2 * width_k)
    own_y = lax.axis_index(Y)
    places = jnp.arange(y_size, dtype=jnp.int32)
    numbers = jnp.arange(local_count, dtype=jnp.int32)
    column_slots = (
        ((own_y - places[:, None]) % y_size * z_size + lax.axis_index(Z)) * local_count + numbers
    ).reshape(-1)

    def packed_out(after):
        weights = (jnp.swapaxes(output_down_weight, 1, 2), output_up_weight)
        width = sum(weight.shape[2] for weight in weights)
        shape = (local_count, rank, width)
        return call(pack, shape, jnp.bfloat16, *weights, scalars=0, after=after)

    def shifted(page, k):
        return lax.ppermute(page, Y, [(i, (i + k) % y_size) for i in range(y_size)])

    z_blocks = pl.pallas_call(
        first_blocks,
        out_shape=jax.ShapeDtypeStruct((z_size, local_rows, local_width + 128), jnp.bfloat16),
        in_specs=[ANY] * 3,
        out_specs=VMEM,
        scratch_shapes=[
            pltpu.SMEM(adapter_id.shape, jnp.int32),
            pltpu.SMEM(adapter_slot.shape, jnp.int32),
            pltpu.VMEM(hidden.shape, jnp.bfloat16),
            pltpu.SemaphoreType.DMA((3,)),
        ],
    )(adapter_id, adapter_slot, hidden)
    y_blocks = call(
        second_blocks,
        (y_size, z_size * local_rows, local_width + 128),
        jnp.bfloat16,
        exchange(z_blocks, Z),
        scalars=0,
    )
    z_rows = y_blocks[0]
    all_rows = exchange(y_blocks, Y).reshape(y_size * z_size * local_rows, -1)

    early = packed_out((y_blocks,))
    near = [shifted(early, 1)]
    packed_shape = (t_size, all_rows.shape[0] // t_size * 3 // 2, 2 * rank)
    part = call(
        down_first,
        packed_shape,
        jnp.float32,
        column_slots,
        all_rows,
        jnp.swapaxes(query_key_value_down, 1, 2),
    )
    ranks = exchange(
        call(rank_blocks, packed_shape, jnp.bfloat16, exchange(part, T), scalars=0, after=near), T
    )
    delta = call(
        up_first,
        (all_rows.shape[0], cuts[3]),
        jnp.bfloat16,
        column_slots,
        ranks,
        all_rows,
        query_up_weight,
        key_up_weight,
        value_up_weight,
    )
    from_y = exchange(delta.reshape(y_size, z_size * local_rows, cuts[3]), Y)
    terms = exchange(
        call(term_blocks, (z_size, local_rows, cuts[3]), jnp.bfloat16, from_y, scalars=0), Z
    )
    late = packed_out((from_y,))
    out_pages = [early, near[0], shifted(late, 2), shifted(late, 3)]
    attention, out_blocks = pl.pallas_call(
        attend,
        out_shape=[
            jax.ShapeDtypeStruct(q_base.shape, jnp.bfloat16),
            jax.ShapeDtypeStruct((z_size,) + q_base.shape, jnp.bfloat16),
        ],
        in_specs=[ANY] * 8,
        out_specs=[VMEM] * 2,
        scratch_shapes=[
            pltpu.SMEM(page_table.shape, jnp.int32),
            pltpu.SMEM(context_len.shape, jnp.int32),
            pltpu.VMEM(terms.shape, jnp.bfloat16),
            pltpu.VMEM(q_base.shape, jnp.bfloat16),
            pltpu.VMEM(base_key.shape, jnp.bfloat16),
            pltpu.VMEM(base_value.shape, jnp.bfloat16),
            pltpu.VMEM(paged_key_cache.shape, jnp.bfloat16),
            pltpu.VMEM(paged_value_cache.shape, jnp.bfloat16),
            pltpu.SemaphoreType.DMA((8,)),
        ],
        compiler_params=pltpu.CompilerParams(vmem_limit_bytes=52 * 2**20),
    )(
        page_table,
        context_len,
        terms,
        q_base,
        base_key,
        base_value,
        paged_key_cache,
        paged_value_cache,
    )
    out_rows = exchange(out_blocks, Z).reshape(z_size * local_rows, -1)
    sides = call(
        make_down_second(0),
        (t_size, z_size * local_rows // 2, 2 * rank),
        jnp.float32,
        column_slots,
        out_rows,
        z_rows,
        *out_pages,
    )
    term = call(
        make_up_second(local_width),
        (z_size * local_rows, output_up_weight.shape[2]),
        jnp.bfloat16,
        column_slots,
        exchange(sides, T),
        z_rows,
        *out_pages,
    )
    output_adapter_term = to_requests(term)
    return (attention, output_adapter_term.astype(jnp.bfloat16))


def solution(mesh):
    chips_y = 4
    wide, tensor = mesh.devices.shape
    devices = np.asarray(mesh.devices).reshape(chips_y, wide // chips_y, tensor)
    W = (Y, Z)
    return jax.shard_map(
        body,
        mesh=Mesh(devices, (Y, Z, T)),
        in_specs=(
            P(W, T),
            P(W, T),
            P(W, T),
            P(W, T),
            P(W, None, T),
            P(W, None, T),
            P(W, None),
            P(W),
            P(W),
            P(),
            P(W, T, None),
            P(W, None, T),
            P(W, None, T),
            P(W, None, T),
            P(W, T, None),
            P(W, None, T),
        ),
        out_specs=(P(W, T), P(W, T)),
        check_vma=False,
    )
```

```python
import jax
import jax.numpy as jnp
import numpy as np
from jax import lax
from jax.experimental import pallas as pl
from jax.experimental.pallas import tpu as pltpu
from jax.sharding import Mesh, PartitionSpec as P

adapter_scale = 2.0
Y, Z, T = "y", "z", "tensor"


def exchange(blocks, axis):
    return lax.all_to_all(blocks, axis, 0, 0)


def spread(block, axis):
    copies = jnp.broadcast_to(block[None], (lax.axis_size(axis),) + block.shape)
    return exchange(copies, axis)


def summed(parts):
    return jnp.sum(parts.astype(jnp.float32), axis=0)


NT = (((1,), (1,)), ((), ()))
VMEM = pl.BlockSpec(memory_space=pltpu.VMEM)
SMEM = pl.BlockSpec(memory_space=pltpu.SMEM)


ANY = pl.BlockSpec(memory_space=pl.ANY)


def call(kernel, shape, dtype, *operands, scalars=1, after=()):
    count = len(operands)

    def run(*refs):
        kernel(*refs[:count], *refs[count + len(after) :])

    return pl.pallas_call(
        run,
        out_shape=jax.ShapeDtypeStruct(shape, dtype),
        in_specs=[SMEM] * scalars + [VMEM] * (count - scalars) + [ANY] * len(after),
        out_specs=VMEM,
        compiler_params=pltpu.CompilerParams(vmem_limit_bytes=32 * 2**20),
    )(*operands, *after)


def fetch(sources, targets, sems):
    copies = [
        pltpu.make_async_copy(source, target, sems.at[i])
        for i, (source, target) in enumerate(zip(sources, targets))
    ]
    for copy in copies:
        copy.start()
    return copies


def first_blocks(id_hbm, slot_hbm, hidden_hbm, out_ref, id_ref, slot_ref, hidden_ref, sems):
    for copy in fetch((id_hbm, slot_hbm, hidden_hbm), (id_ref, slot_ref, hidden_ref), sems):
        copy.wait()
    rows, width = hidden_ref.shape
    tags = [
        jnp.full((1, 128), slot_ref[id_ref[r]].astype(jnp.float32), jnp.float32) for r in range(rows)
    ]
    block = jnp.concatenate(
        [hidden_ref[...], jnp.concatenate(tags, axis=0).astype(jnp.bfloat16)], axis=1
    )
    for z in range(out_ref.shape[0]):
        out_ref[z] = block


def attend(*refs):
    keys_ref, sources, (out_ref, block_ref), held, sems = (
        refs[0],
        refs[1:8],
        refs[8:10],
        refs[10:17],
        refs[17],
    )
    table_ref, length_ref, terms_ref, q_ref, k_ref, v_ref, values_ref = held
    copies = fetch(sources, held, sems)
    for copy in copies[:6]:
        copy.wait()
    rows, width_q = q_ref.shape
    size = k_ref.shape[1]
    heads = width_q // size
    delta = summed(terms_ref[...])
    parts = (
        q_ref[...].astype(jnp.float32) + delta[:, :width_q],
        k_ref[...].astype(jnp.float32) + delta[:, width_q : width_q + size],
        v_ref[...].astype(jnp.float32) + delta[:, width_q + size :],
    )
    query, key, value = [part.astype(jnp.bfloat16).astype(jnp.float32) for part in parts]
    inverse = 1.0 / size**0.5
    done = []
    for r in range(rows):
        pages = [table_ref[r, i] for i in range(table_ref.shape[1])]
        q = jnp.concatenate(
            [query[r : r + 1, h * size : (h + 1) * size] for h in range(heads)], axis=0
        )
        keys = jnp.concatenate([keys_ref[page] for page in pages], axis=0)
        scores = lax.dot_general(
            q.astype(jnp.bfloat16), keys, NT, preferred_element_type=jnp.float32
        )
        live = lax.broadcasted_iota(jnp.int32, scores.shape, 1) < length_ref[r]
        scores = jnp.where(live, scores * inverse, jnp.float32(-1e30))
        own = jnp.sum(q * key[r : r + 1], axis=1, keepdims=True) * inverse
        top = jnp.maximum(jnp.max(scores, axis=1, keepdims=True), own)
        weights = jnp.where(live, jnp.exp(scores - top), 0.0)
        own_weight = jnp.exp(own - top)
        total = jnp.sum(weights, axis=1, keepdims=True) + own_weight
        if r == 0:
            copies[6].wait()
        values = jnp.concatenate([values_ref[page] for page in pages], axis=0)
        mixed = jnp.dot(weights.astype(jnp.bfloat16), values, preferred_element_type=jnp.float32)
        own_rounded = own_weight.astype(jnp.bfloat16).astype(jnp.float32)
        mixed = (mixed + own_rounded * value[r : r + 1]) / total
        done.append(jnp.concatenate([mixed[h : h + 1] for h in range(heads)], axis=1))
    attention = jnp.concatenate(done, axis=0).astype(jnp.bfloat16)
    out_ref[...] = attention
    for z in range(block_ref.shape[0]):
        block_ref[z] = attention


def second_blocks(from_z_ref, out_ref):
    rows = from_z_ref[...].reshape(out_ref.shape[1:])
    for y in range(out_ref.shape[0]):
        out_ref[y] = rows


def pack(*refs):
    out_ref, at = refs[-1], 0
    for ref in refs[:-1]:
        out_ref[:, :, at : at + ref.shape[2]] = ref[...]
        at += ref.shape[2]


def picked(slots_ref, tags, values, number):
    return jnp.where(tags == slots_ref[number].astype(jnp.float32), values, jnp.zeros_like(values))


def write_packed(ranks, out_ref):
    shares, packed_rows, lanes = out_ref.shape
    rows = ranks.shape[0] // shares
    half = packed_rows - rows
    for t in range(shares):
        share = ranks[t * rows : (t + 1) * rows]
        out_ref[t, :rows] = share[:, :lanes]
        out_ref[t, rows:] = jnp.concatenate(
            [share[:half, lanes:], share[half:, lanes:]], axis=1
        )


def read_packed(ref):
    shares, packed_rows, lanes = ref.shape
    rows = packed_rows * 2 // 3
    first, last = [], []
    for t in range(shares):
        share = ref[t].astype(jnp.float32)
        first.append(share[:rows])
        last += [share[rows:, : lanes // 2], share[rows:, lanes // 2 :]]
    return jnp.concatenate([jnp.concatenate(first, 0), jnp.concatenate(last, 0)], axis=1)


def rank_blocks(shares_ref, out_ref):
    ranks = jnp.sum(shares_ref[...], axis=0).astype(jnp.bfloat16)
    for t in range(out_ref.shape[0]):
        out_ref[t] = ranks


def down_first(slots_ref, rows_ref, weight_ref, out_ref):
    width = weight_ref.shape[2]
    rows, tags = rows_ref[:, :width], rows_ref[:, width : width + 1].astype(jnp.float32)
    total = None
    for j in range(weight_ref.shape[0]):
        product = lax.dot_general(rows, weight_ref[j], NT, preferred_element_type=jnp.float32)
        mine = picked(slots_ref, tags, product, j)
        total = mine if total is None else total + mine
    write_packed(total, out_ref)


def tags_of(rows_ref, at, width):
    return rows_ref[:, at : at + width].astype(jnp.float32)


def grown(slots_ref, tags, ranks, pages, at, width):
    total = None
    for k, page in enumerate(pages):
        count, rank, _ = page.shape
        mine = [picked(slots_ref, tags, ranks, k * count + j) for j in range(count)]
        product = jnp.dot(
            jnp.concatenate(mine, axis=1).astype(jnp.bfloat16),
            page[:, :, at : at + width].reshape(count * rank, width),
            preferred_element_type=jnp.float32,
        )
        total = product if total is None else total + product
    return (adapter_scale * total).astype(jnp.bfloat16)


def up_first(slots_ref, ranks_ref, rows_ref, q_up, k_up, v_up, out_ref):
    rank = q_up.shape[1]
    tags = tags_of(rows_ref, rows_ref.shape[1] - 128, rank)
    ranks = read_packed(ranks_ref)
    at = 0
    for i, page in enumerate((q_up, k_up, v_up)):
        width = page.shape[2]
        mine = ranks[:, i * rank : (i + 1) * rank]
        out_ref[:, at : at + width] = grown(slots_ref, tags, mine, [page], 0, width)
        at += width


def term_blocks(from_y_ref, out_ref):
    out_ref[...] = summed(from_y_ref[...]).reshape(out_ref.shape).astype(jnp.bfloat16)


def make_down_second(at):
    def down_second(slots_ref, out_rows_ref, rows_ref, *refs):
        pages, out_ref = refs[:-1], refs[-1]
        count, rank, _ = pages[0].shape
        rows = out_rows_ref[...]
        tags = tags_of(rows_ref, rows_ref.shape[1] - 128, rank)
        total = jnp.zeros((rows.shape[0], rank), jnp.float32)
        for k, page in enumerate(pages):
            for j in range(count):
                weight = page[j, :, at : at + rows.shape[1]]
                product = lax.dot_general(rows, weight, NT, preferred_element_type=jnp.float32)
                total = total + picked(slots_ref, tags, product, k * count + j)
        half = rows.shape[0] // 2
        side = jnp.concatenate([total[:half], total[half:]], axis=1)
        for t in range(out_ref.shape[0]):
            out_ref[t] = side

    return down_second


def make_up_second(at):
    def up_second(slots_ref, parts_ref, rows_ref, *refs):
        pages, out_ref = refs[:-1], refs[-1]
        rank = pages[0].shape[1]
        side = jnp.sum(parts_ref[...], axis=0).astype(jnp.bfloat16).astype(jnp.float32)
        ranks = jnp.concatenate([side[:, :rank], side[:, rank:]], axis=0)
        tags = tags_of(rows_ref, rows_ref.shape[1] - 128, rank)
        out_ref[...] = grown(slots_ref, tags, ranks, pages, at, out_ref.shape[1])

    return up_second


def to_requests(rows):
    return summed(exchange(rows.reshape(lax.axis_size(Z), -1, rows.shape[1]), Z))


def body(
    hidden,
    q_base,
    base_key,
    base_value,
    paged_key_cache,
    paged_value_cache,
    page_table,
    context_len,
    adapter_id,
    adapter_slot,
    query_key_value_down,
    query_up_weight,
    key_up_weight,
    value_up_weight,
    output_down_weight,
    output_up_weight,
):
    local_rows, local_width = hidden.shape
    local_count = query_key_value_down.shape[0]
    y_size, z_size, t_size = lax.axis_size(Y), lax.axis_size(Z), lax.axis_size(T)
    rank, width_q, width_k = query_up_weight.shape[1], q_base.shape[1], base_key.shape[1]
    cuts = (0, width_q, width_q + width_k, width_q + 2 * width_k)
    own_y = lax.axis_index(Y)
    places = jnp.arange(y_size, dtype=jnp.int32)
    numbers = jnp.arange(local_count, dtype=jnp.int32)
    column_slots = (
        ((own_y - places[:, None]) % y_size * z_size + lax.axis_index(Z)) * local_count + numbers
    ).reshape(-1)

    def packed_out(after):
        weights = (jnp.swapaxes(output_down_weight, 1, 2), output_up_weight)
        width = sum(weight.shape[2] for weight in weights)
        shape = (local_count, rank, width)
        return call(pack, shape, jnp.bfloat16, *weights, scalars=0, after=after)

    def shifted(page, k):
        return lax.ppermute(page, Y, [(i, (i + k) % y_size) for i in range(y_size)])

    z_blocks = pl.pallas_call(
        first_blocks,
        out_shape=jax.ShapeDtypeStruct((z_size, local_rows, local_width + 128), jnp.bfloat16),
        in_specs=[ANY] * 3,
        out_specs=VMEM,
        scratch_shapes=[
            pltpu.SMEM(adapter_id.shape, jnp.int32),
            pltpu.SMEM(adapter_slot.shape, jnp.int32),
            pltpu.VMEM(hidden.shape, jnp.bfloat16),
            pltpu.SemaphoreType.DMA((3,)),
        ],
    )(adapter_id, adapter_slot, hidden)
    y_blocks = call(
        second_blocks,
        (y_size, z_size * local_rows, local_width + 128),
        jnp.bfloat16,
        exchange(z_blocks, Z),
        scalars=0,
    )
    z_rows = y_blocks[0]
    all_rows = exchange(y_blocks, Y).reshape(y_size * z_size * local_rows, -1)

    early = packed_out((y_blocks,))
    near = [shifted(early, 1)]
    packed_shape = (t_size, all_rows.shape[0] // t_size * 3 // 2, 2 * rank)
    part = call(
        down_first,
        packed_shape,
        jnp.float32,
        column_slots,
        all_rows,
        jnp.swapaxes(query_key_value_down, 1, 2),
    )
    ranks = exchange(
        call(rank_blocks, packed_shape, jnp.bfloat16, exchange(part, T), scalars=0, after=near), T
    )
    delta = call(
        up_first,
        (all_rows.shape[0], cuts[3]),
        jnp.bfloat16,
        column_slots,
        ranks,
        all_rows,
        query_up_weight,
        key_up_weight,
        value_up_weight,
    )
    from_y = exchange(delta.reshape(y_size, z_size * local_rows, cuts[3]), Y)
    terms = exchange(
        call(term_blocks, (z_size, local_rows, cuts[3]), jnp.bfloat16, from_y, scalars=0), Z
    )
    late = packed_out((from_y,))
    out_pages = [early, near[0], shifted(late, 2), shifted(late, 3)]
    attention, out_blocks = pl.pallas_call(
        attend,
        out_shape=[
            jax.ShapeDtypeStruct(q_base.shape, jnp.bfloat16),
            jax.ShapeDtypeStruct((z_size,) + q_base.shape, jnp.bfloat16),
        ],
        in_specs=[VMEM] + [ANY] * 7,
        out_specs=[VMEM] * 2,
        scratch_shapes=[
            pltpu.SMEM(page_table.shape, jnp.int32),
            pltpu.SMEM(context_len.shape, jnp.int32),
            pltpu.VMEM(terms.shape, jnp.bfloat16),
            pltpu.VMEM(q_base.shape, jnp.bfloat16),
            pltpu.VMEM(base_key.shape, jnp.bfloat16),
            pltpu.VMEM(base_value.shape, jnp.bfloat16),
            pltpu.VMEM(paged_value_cache.shape, jnp.bfloat16),
            pltpu.SemaphoreType.DMA((7,)),
        ],
        compiler_params=pltpu.CompilerParams(vmem_limit_bytes=52 * 2**20),
    )(
        paged_key_cache,
        page_table,
        context_len,
        terms,
        q_base,
        base_key,
        base_value,
        paged_value_cache,
    )
    out_rows = exchange(out_blocks, Z).reshape(z_size * local_rows, -1)
    sides = call(
        make_down_second(0),
        (t_size, z_size * local_rows // 2, 2 * rank),
        jnp.float32,
        column_slots,
        out_rows,
        z_rows,
        *out_pages,
    )
    term = call(
        make_up_second(local_width),
        (z_size * local_rows, output_up_weight.shape[2]),
        jnp.bfloat16,
        column_slots,
        exchange(sides, T),
        z_rows,
        *out_pages,
    )
    output_adapter_term = to_requests(term)
    return (attention, output_adapter_term.astype(jnp.bfloat16))


def solution(mesh):
    chips_y = 4
    wide, tensor = mesh.devices.shape
    devices = np.asarray(mesh.devices).reshape(chips_y, wide // chips_y, tensor)
    W = (Y, Z)
    return jax.shard_map(
        body,
        mesh=Mesh(devices, (Y, Z, T)),
        in_specs=(
            P(W, T),
            P(W, T),
            P(W, T),
            P(W, T),
            P(W, None, T),
            P(W, None, T),
            P(W, None),
            P(W),
            P(W),
            P(),
            P(W, T, None),
            P(W, None, T),
            P(W, None, T),
            P(W, None, T),
            P(W, T, None),
            P(W, None, T),
        ),
        out_specs=(P(W, T), P(W, T)),
        check_vma=False,
    )
```
